512 devices in a mesh: store: 8 (over y), ctx: 16 (over z, core), tensor: 4 (over x).
Axes of the slice: x: 4, y: 8, z: 8, core: 2. Of those that a mesh axis runs over, the one named last changes fastest.
Arguments:
- queries: bfloat16 [65536, 4096], P(('store', 'ctx', 'tensor')), may hold values from -21 to 21
- grad_out: bfloat16 [65536, 4096], P(('store', 'ctx', 'tensor')), may hold values from -6 to 6
- attn_out: bfloat16 [65536, 4096], P(('store', 'ctx', 'tensor')), may hold values from -3 to 3
- passage_keys: bfloat16 [512, 16, 512], P(('store', 'ctx'), None, 'tensor'), may hold values from -9 to 9
- passage_values: bfloat16 [512, 16, 512], P(('store', 'ctx'), None, 'tensor'), may hold values from -6 to 6
- block_lists: int32 [512, 16], replicated, may hold values from 0 to 511, as said below
- passage_lengths: int32 [512], replicated, may hold values from 4 to 16, as said below
Outputs:
- query_grad: bfloat16 [65536, 4096], P(('store', 'ctx', 'tensor'))
- key_grad: bfloat16 [512, 16, 512], P(('store', 'ctx'), None, 'tensor')
- value_grad: bfloat16 [512, 16, 512], P(('store', 'ctx'), None, 'tensor')
The draws below stay inside these ranges and needn't reach their ends.
Inputs may be any that keep to these rules, and one draw needn't show every extreme that they name: `block_lists`: passage p belongs to owner floor(p / 4). The rows of query shard c (rows c * 4 to (c + 1) * 4 - 1) together name 64 passages of as many different owners. `passage_lengths`: some passage has exactly 16 live slots.
All inputs are finite; a program needn't handle non-finite values.
Results may differ from the reference program's by a relative error of at most 0.02.
Values may be sent and summed in bfloat16 or wider, within the bound.
No kernel may reach another device: no remote copies, remote signals or barrier semaphores. Data moves between devices by JAX's collectives and lax.ppermute only.
A program may use at most 64 MiB of HBM per device.

```python
import jax
import jax.numpy as jnp
from jax import lax

H = 32
KVH = 4
DH = 128
D = 4096
GROUP = 8
QBLK = 128
PLEN = 16
PASS_DEV = 4
OWNERS = 128
PASSAGES = 512
TOKENS = 65536
BLOCKS_DEV = 4
BLOCKS = 512
LIST = 16


def shared_lists(key):
    source = jax.random.fold_in(key, 902)
    first_key, second_key = jax.random.split(source)
    per_shard = BLOCKS_DEV * LIST
    passage_pick = jax.random.randint(first_key, (OWNERS, per_shard), 0, PASS_DEV)
    shard_keys = jax.random.split(second_key, OWNERS)
    owners_listed = jax.vmap(lambda one_key: jax.random.permutation(one_key, OWNERS)[:per_shard])(shard_keys)
    return (owners_listed * PASS_DEV + passage_pick).reshape(BLOCKS, LIST).astype(jnp.int32)


def draw_block_lists(key, part):
    listed = shared_lists(key)
    return listed


def draw_queries(key, part):
    key = jax.random.fold_in(key, 3)
    return jax.random.truncated_normal(key, -4.0, 4.0, (TOKENS, H * DH), jnp.float32).astype(jnp.bfloat16)


def draw_passage_keys(key, part):
    key = jax.random.fold_in(key, 5)
    return jax.random.truncated_normal(key, -4.0, 4.0, (PASSAGES, PLEN, KVH * DH), jnp.float32).astype(jnp.bfloat16)


def draw_passage_lengths(key, part):
    key = jax.random.fold_in(key, 7)
    first_key, second_key = jax.random.split(key)
    raw_lengths = jax.random.randint(first_key, (PASSAGES,), PLEN // 4, PLEN + 1)
    longest = jax.random.randint(second_key, (), 0, PASSAGES)
    return jnp.where(jnp.arange(PASSAGES) == longest, PLEN, raw_lengths).astype(jnp.int32)


def block_scale(key, dims, shards, smallest, top_value):
    def one(dim, shards_of):
        steps = jax.random.uniform(jax.random.fold_in(jax.random.fold_in(key, 6), dim), (shards_of,), jnp.float32, smallest / len(shards), top_value / len(shards))
        return jnp.repeat(jnp.exp(steps), dims[dim] // shards_of).reshape((-1,) + (1,) * (len(dims) - dim - 1))

    loudness = one(*shards[0])
    for cut in shards[1:]:
        loudness = loudness * one(*cut)
    return loudness


def gaussian(stream_key, extent, width, limit, shards=(), held_as=jnp.bfloat16):
    loudness = block_scale(stream_key, extent, shards, -0.22, 0.18) if shards else 1.0
    values = jax.random.normal(stream_key, extent, jnp.float32) * width * loudness
    return jnp.minimum(jnp.maximum(values, -limit), limit).astype(held_as)


def setup_inputs(seed: int = 0) -> dict:
    key_of = jax.random.split(jax.random.key(seed), 8)
    return {
        "queries": draw_queries(jax.random.fold_in(key_of[7], 71), 0),
        "grad_out": gaussian(key_of[1], (TOKENS, D), 1.0, 6.0, ((0, 512),)),
        "attn_out": gaussian(key_of[2], (TOKENS, D), 0.5, 3.0, ((0, 512),)),
        "passage_keys": draw_passage_keys(jax.random.fold_in(key_of[7], 71), 0),
        "passage_values": gaussian(key_of[4], (PASSAGES, PLEN, KVH * DH), 1.0, 6.0, ((0, 128), (2, 4))),
        "block_lists": draw_block_lists(jax.random.fold_in(key_of[7], 71), 0),
        "passage_lengths": draw_passage_lengths(jax.random.fold_in(key_of[7], 71), 0),
    }


def group_backward(q_group, grad_group, out_group, key_group, value_group, live_mask):
    key_scale = DH ** -0.5
    queries32 = q_group.astype(jnp.float32)
    grads32 = grad_group.astype(jnp.float32)
    keys32 = key_group.astype(jnp.float32)
    values32 = value_group.astype(jnp.float32)
    scores = jnp.einsum("hqd,kd->hqk", queries32, keys32) * key_scale
    masked = jnp.where(live_mask[None, None, :], scores, jnp.float32(-1e30))
    row_top = jnp.max(masked, axis=2, keepdims=True)
    row_total = jnp.sum(jnp.where(live_mask[None, None, :], jnp.exp(masked - row_top), jnp.float32(0.0)), axis=2, keepdims=True)
    log_total = row_top + jnp.log(row_total)
    weights = jnp.where(live_mask[None, None, :], jnp.exp(scores - log_total), jnp.float32(0.0))
    weights_half = weights.astype(jnp.bfloat16)
    row_delta = jnp.sum(grads32 * out_group.astype(jnp.float32), axis=2, keepdims=True)
    weight_grads = jnp.einsum("hqd,kd->hqk", grads32, values32)
    score_grads = (weights * (weight_grads - row_delta)).astype(jnp.bfloat16).astype(jnp.float32)
    query_part = jnp.einsum("hqk,kd->hqd", score_grads, keys32) * key_scale
    key_part = jnp.einsum("hqk,hqd->kd", score_grads, queries32) * key_scale
    value_part = jnp.einsum("hqk,hqd->kd", weights_half.astype(jnp.float32), grads32)
    return query_part, key_part, value_part


def head_major(block_rows):
    return block_rows.reshape(QBLK, KVH, GROUP, DH).transpose(1, 2, 0, 3)


def reference(queries, grad_out, attn_out, passage_keys, passage_values, block_lists, passage_lengths):
    key_width = KVH * DH
    slot_ids = jnp.arange(PLEN, dtype=jnp.int32)

    def block_step(running, block_index):
        key_total, value_total = running
        row_start = (block_index * QBLK).astype(jnp.int32)
        q_block = head_major(lax.dynamic_slice_in_dim(queries, row_start, QBLK, 0))
        grad_block = head_major(lax.dynamic_slice_in_dim(grad_out, row_start, QBLK, 0))
        out_block = head_major(lax.dynamic_slice_in_dim(attn_out, row_start, QBLK, 0))
        listed = lax.dynamic_index_in_dim(block_lists, block_index.astype(jnp.int32), 0, keepdims=False).astype(jnp.int32)
        key_rows = passage_keys[listed].reshape(LIST * PLEN, KVH, DH).transpose(1, 0, 2)
        value_rows = passage_values[listed].reshape(LIST * PLEN, KVH, DH).transpose(1, 0, 2)
        live_mask = (slot_ids[None, :] < passage_lengths[listed][:, None]).reshape(LIST * PLEN)

        def per_group(items):
            return group_backward(items[0], items[1], items[2], items[3], items[4], live_mask)

        query_part, key_part, value_part = lax.map(per_group, (q_block, grad_block, out_block, key_rows, value_rows))
        query_rows = query_part.transpose(2, 0, 1, 3).reshape(QBLK, H * DH)
        key_part = key_part.reshape(KVH, LIST, PLEN, DH).transpose(1, 2, 0, 3).reshape(LIST, PLEN, key_width)
        value_part = value_part.reshape(KVH, LIST, PLEN, DH).transpose(1, 2, 0, 3).reshape(LIST, PLEN, key_width)
        key_total = key_total.at[listed].add(lax.optimization_barrier(key_part.astype(jnp.bfloat16)).astype(jnp.float32))
        value_total = value_total.at[listed].add(lax.optimization_barrier(value_part.astype(jnp.bfloat16)).astype(jnp.float32))
        return (key_total, value_total), query_rows.astype(jnp.bfloat16)

    start = (jnp.zeros((PASSAGES, PLEN, key_width), jnp.float32), jnp.zeros((PASSAGES, PLEN, key_width), jnp.float32))
    totals, query_blocks = lax.scan(block_step, start, jnp.arange(BLOCKS, dtype=jnp.int32))
    query_grad = query_blocks.reshape(TOKENS, H * DH)
    return query_grad, totals[0].astype(jnp.bfloat16), totals[1].astype(jnp.bfloat16)
```

```python
import jax
import jax.numpy as jnp
from jax import lax
from jax.experimental import pallas as pl
from jax.experimental.pallas import tpu as pltpu
from jax.sharding import PartitionSpec as P

DH = 128
QBLK = 128
BF16 = jnp.bfloat16
F32 = jnp.float32
MASKED = -1e30
NT = (((1,), (1,)), ((), ()))
TN = (((0,), (0,)), ((), ()))
VMEM_LIMIT = 48 * 1024 * 1024


def vmem():
    return pl.BlockSpec(memory_space=pltpu.VMEM)


def smem():
    return pl.BlockSpec(memory_space=pltpu.SMEM)


def params():
    return pltpu.CompilerParams(vmem_limit_bytes=VMEM_LIMIT)


def send_kernel(pick_ref, keys_ref, values_ref, out_ref):
    plen = keys_ref.shape[1]

    def body(n, carry):
        k = jnp.maximum(pick_ref[n], 0)
        out_ref[n, 0:plen, :] = keys_ref[k]
        out_ref[n, plen : 2 * plen, :] = values_ref[k]
        return carry

    lax.fori_loop(0, out_ref.shape[0], body, 0, unroll=8)


def prep_kernel(place_ref, q_ref, g_ref, o_ref, *rest):
    *message_refs, delta_ref = rest
    parts = len(message_refs)
    width = q_ref.shape[1] // parts
    heads = q_ref.shape[1] // DH
    share = heads // parts
    lane = lax.broadcasted_iota(jnp.int32, (QBLK, DH), 1)
    delta = jnp.zeros((QBLK, DH), F32)
    for h in range(heads):
        cols = slice(h * DH, (h + 1) * DH)
        term = jnp.sum(g_ref[:, cols].astype(F32) * o_ref[:, cols].astype(F32), axis=1, keepdims=True)
        delta = jnp.where(lane == h, term, delta)
    delta_ref[...] = delta.T
    for j, message_ref in enumerate(message_refs):
        to = lax.rem(place_ref[0] + j, parts)
        cols = pl.ds(pl.multiple_of(to * width, width), width)
        message_ref[0:QBLK, :] = q_ref[:, cols]
        message_ref[QBLK : 2 * QBLK, :] = g_ref[:, cols]
        rows = delta_ref[pl.ds(pl.multiple_of(to * share, share), share), :]
        high = rows.astype(BF16).astype(F32)
        message_ref[2 * QBLK : 2 * QBLK + 2 * share, :] = jnp.zeros((2 * share, width), BF16)
        message_ref[2 * QBLK : 2 * QBLK + 2 * share, 0:DH] = jnp.concatenate(
            [high, rows - high], axis=0
        ).astype(BF16)


def main_kernel(place_ref, lists_ref, lengths_ref, pass_dev, incoming_ref, *rest):
    parts = lists_ref.shape[0]
    message_refs = rest[:parts]
    dq_refs = rest[parts : 2 * parts]
    out_ref, k_ref, v_ref, bias_ref = rest[2 * parts :]
    list_len = lists_ref.shape[1]
    plen = incoming_ref.shape[1] // 2
    width = message_refs[0].shape[1]
    share = width // DH
    scale = DH ** (-0.5)
    out_ref[...] = jnp.zeros_like(out_ref)
    slot_row = lax.broadcasted_iota(jnp.int32, (plen, DH), 0)
    for j, (message_ref, dq_ref) in enumerate(zip(message_refs, dq_refs)):
        block = lax.rem(place_ref[0] + parts - j, parts)
        owners = []
        for p in range(list_len):
            passage = lists_ref[block, p]
            owner = passage // pass_dev
            owners.append(owner)
            rows = slice(p * plen, (p + 1) * plen)
            k_ref[rows, :] = incoming_ref[owner, 0:plen, :]
            v_ref[rows, :] = incoming_ref[owner, plen : 2 * plen, :]
            bias_ref[rows, :] = jnp.where(slot_row < lengths_ref[passage], 0.0, MASKED)
        keys = k_ref[...]
        values = v_ref[...]
        heads = [slice(h * DH, (h + 1) * DH) for h in range(share)]
        queries = jnp.concatenate([message_ref[0:QBLK, c] for c in heads], axis=0)
        grads = jnp.concatenate([message_ref[QBLK : 2 * QBLK, c] for c in heads], axis=0)
        delta_parts = message_ref[2 * QBLK : 2 * QBLK + 2 * share, 0:DH].astype(F32)
        delta = delta_parts[:share] + delta_parts[share:]
        delta = jnp.concatenate([delta[h : h + 1] for h in range(share)], axis=1)
        bias = jnp.concatenate([bias_ref[...]] * share, axis=1)
        scores = lax.dot_general(keys, queries, NT, preferred_element_type=F32) * scale + bias
        weights = jnp.exp(scores - jnp.max(scores, axis=0, keepdims=True))
        weights = weights * (1.0 / jnp.sum(weights, axis=0, keepdims=True))
        weight_grads = lax.dot_general(values, grads, NT, preferred_element_type=F32)
        score_grads = (weights * (weight_grads - delta)).astype(BF16)
        value_term = jnp.dot(weights.astype(BF16), grads, preferred_element_type=F32).astype(BF16)
        key_term = (jnp.dot(score_grads, queries, preferred_element_type=F32) * scale).astype(BF16)
        for p, owner in enumerate(owners):
            rows = slice(p * plen, (p + 1) * plen)
            out_ref[owner, 0:plen, :] = key_term[rows]
            out_ref[owner, plen : 2 * plen, :] = value_term[rows]
        query_part = lax.dot_general(keys, score_grads, TN, preferred_element_type=F32) * scale
        for c in heads:
            dq_ref[:, c] = query_part[:, c].T.astype(BF16)


def place_kernel(place_ref, *rest):
    *piece_refs, out_ref, sems = rest
    parts = len(piece_refs)
    width = out_ref.shape[1] // parts
    copies = []
    for j, piece_ref in enumerate(piece_refs):
        to = lax.rem(place_ref[0] + j, parts)
        cols = pl.ds(pl.multiple_of(to * width, width), width)
        copies.append(pltpu.make_async_copy(piece_ref, out_ref.at[:, cols], sems.at[j]))
    for copy in copies:
        copy.start()
    for copy in copies:
        copy.wait()


def sum_kernel(pick_ref, terms_ref, keys_ref, values_ref):
    pass_dev, plen, _ = keys_ref.shape

    def body(n, sums):
        k = pick_ref[n]
        term = terms_ref[n].astype(F32)
        return tuple(s + jnp.where(k == i, term, 0.0) for i, s in enumerate(sums))

    zero = jnp.zeros((2 * plen, DH), F32)
    sums = lax.fori_loop(0, terms_ref.shape[0], body, (zero,) * pass_dev, unroll=8)
    for i, s in enumerate(sums):
        keys_ref[i] = s[:plen].astype(BF16)
        values_ref[i] = s[plen:].astype(BF16)


def local(queries, grad_out, attn_out, passage_keys, passage_values, block_lists, passage_lengths):
    shards = lax.axis_size("store") * lax.axis_size("ctx")
    parts = lax.axis_size("tensor")
    my_shard = lax.axis_index("store") * lax.axis_size("ctx") + lax.axis_index("ctx")
    place = lax.axis_index("tensor").astype(jnp.int32).reshape(1)
    pass_dev, plen, _ = passage_keys.shape
    rows, columns = queries.shape
    width = columns // parts
    list_len = block_lists.shape[1]
    all_shape = jax.ShapeDtypeStruct((shards, 2 * plen, DH), BF16)

    picked = jnp.where(block_lists // pass_dev == my_shard, block_lists % pass_dev + 1, 0)
    pick = jnp.sum(picked.reshape(shards, parts * list_len), axis=1) - 1

    outgoing = pl.pallas_call(
        send_kernel,
        out_shape=all_shape,
        in_specs=[smem(), vmem(), vmem()],
        out_specs=vmem(),
        compiler_params=params(),
        name="send",
    )(pick, passage_keys, passage_values)
    incoming = lax.all_to_all(outgoing, ("store", "ctx"), split_axis=0, concat_axis=0, tiled=True)

    message = jax.ShapeDtypeStruct((2 * QBLK + 2 * (width // DH), width), BF16)
    messages = pl.pallas_call(
        prep_kernel,
        out_shape=[message] * parts,
        in_specs=[smem(), vmem(), vmem(), vmem()],
        out_specs=[vmem()] * parts,
        scratch_shapes=[pltpu.VMEM((DH, QBLK), F32)],
        compiler_params=params(),
        cost_estimate=pl.CostEstimate(flops=2 * rows * columns, bytes_accessed=10 * rows * columns, transcendentals=0),
        name="prep",
    )(place, queries, grad_out, attn_out)

    def shift(piece, by):
        if by == 0:
            return piece
        return lax.ppermute(piece, "tensor", [(i, (i + by) % parts) for i in range(parts)])

    messages = [shift(piece, j) for j, piece in enumerate(messages)]
    own_lists = lax.dynamic_slice_in_dim(block_lists, my_shard * parts, parts, 0)

    def main(place_ref, lists_ref, lengths_ref, *refs):
        main_kernel(place_ref, lists_ref, lengths_ref, pass_dev, *refs)

    keys = list_len * plen
    pairs = parts * QBLK * (width // DH) * keys
    *query_parts, outgoing_grads = pl.pallas_call(
        main,
        out_shape=[jax.ShapeDtypeStruct((QBLK, width), BF16)] * parts + [all_shape],
        in_specs=[smem(), smem(), smem(), vmem()] + [vmem()] * parts,
        out_specs=[vmem()] * (parts + 1),
        scratch_shapes=[
            pltpu.VMEM((keys, DH), BF16),
            pltpu.VMEM((keys, DH), BF16),
            pltpu.VMEM((keys, DH), F32),
        ],
        compiler_params=params(),
        cost_estimate=pl.CostEstimate(flops=10 * pairs * DH, bytes_accessed=8 * rows * columns, transcendentals=pairs),
        name="attention",
    )(place, own_lists, passage_lengths, incoming, *messages)

    returned = lax.all_to_all(outgoing_grads, ("store", "ctx"), split_axis=0, concat_axis=0, tiled=True)
    query_parts = [shift(piece, (parts - j) % parts) for j, piece in enumerate(query_parts)]
    query_grad = pl.pallas_call(
        place_kernel,
        out_shape=jax.ShapeDtypeStruct((rows, columns), BF16),
        in_specs=[smem()] + [pl.BlockSpec(memory_space=pl.ANY)] * parts,
        out_specs=pl.BlockSpec(memory_space=pl.ANY),
        scratch_shapes=[pltpu.SemaphoreType.DMA((parts,))],
        cost_estimate=pl.CostEstimate(flops=0, bytes_accessed=4 * rows * columns, transcendentals=0),
        name="place",
    )(place, *query_parts)
    grad_shape = jax.ShapeDtypeStruct(passage_keys.shape, BF16)
    key_grad, value_grad = pl.pallas_call(
        sum_kernel,
        out_shape=[grad_shape, grad_shape],
        in_specs=[smem(), vmem()],
        out_specs=[vmem(), vmem()],
        compiler_params=params(),
        name="sum",
    )(pick, returned)
    return query_grad, key_grad, value_grad


def solution(mesh):
    tokens = P(("store", "ctx", "tensor"), None)
    passages = P(("store", "ctx"), None, "tensor")
    return jax.shard_map(
        local,
        mesh=mesh,
        in_specs=(tokens, tokens, tokens, passages, passages, P(), P()),
        out_specs=(tokens, passages, passages),
        check_vma=False,
    )
```

```python
import jax
import jax.numpy as jnp
from jax import lax
from jax.experimental import pallas as pl
from jax.experimental.pallas import tpu as pltpu
from jax.sharding import Mesh
from jax.sharding import PartitionSpec as P

DH = 128
QBLK = 128
BF16 = jnp.bfloat16
F32 = jnp.float32
MASKED = -1e30
NT = (((1,), (1,)), ((), ()))
TN = (((0,), (0,)), ((), ()))
VMEM_LIMIT = 24 * 1024 * 1024


SHARD_AXES = ("y2", "y1", "y0", "z2", "z1", "z0", "core")
EXCHANGE_AXES = ("core", "y0", "z0", "y1", "z1", "y2", "z2")


def slot_of(shard):
    bits = len(SHARD_AXES)
    slot = 0
    for i, name in enumerate(EXCHANGE_AXES):
        bit = (shard >> (bits - 1 - SHARD_AXES.index(name))) & 1
        slot = slot | (bit << (bits - 1 - i))
    return slot


def exchange(pieces):
    return lax.all_to_all(pieces, EXCHANGE_AXES, split_axis=0, concat_axis=0, tiled=True)


def vmem():
    return pl.BlockSpec(memory_space=pltpu.VMEM)


def smem():
    return pl.BlockSpec(memory_space=pltpu.SMEM)


def params():
    return pltpu.CompilerParams(vmem_limit_bytes=VMEM_LIMIT)


def send_kernel(pick_ref, keys_ref, values_ref, out_ref):
    plen = keys_ref.shape[1]

    def body(n, carry):
        k = jnp.maximum(pick_ref[n], 0)
        slot = slot_of(n)
        out_ref[slot, 0:plen, :] = keys_ref[k]
        out_ref[slot, plen : 2 * plen, :] = values_ref[k]
        return carry

    lax.fori_loop(0, out_ref.shape[0], body, 0, unroll=8)


def prep_kernel(place_ref, q_ref, g_ref, o_ref, *rest):
    *message_refs, delta_ref = rest
    parts = len(message_refs)
    width = q_ref.shape[1] // parts
    heads = q_ref.shape[1] // DH
    share = heads // parts
    lane = lax.broadcasted_iota(jnp.int32, (QBLK, DH), 1)
    delta = jnp.zeros((QBLK, DH), F32)
    for h in range(heads):
        cols = slice(h * DH, (h + 1) * DH)
        term = jnp.sum(g_ref[:, cols].astype(F32) * o_ref[:, cols].astype(F32), axis=1, keepdims=True)
        delta = jnp.where(lane == h, term, delta)
    delta_ref[...] = delta.T
    for j, message_ref in enumerate(message_refs):
        to = lax.rem(place_ref[0] + j, parts)
        cols = pl.ds(pl.multiple_of(to * width, width), width)
        message_ref[0:QBLK, :] = q_ref[:, cols]
        message_ref[QBLK : 2 * QBLK, :] = g_ref[:, cols]
        rows = delta_ref[pl.ds(pl.multiple_of(to * share, share), share), :]
        high = rows.astype(BF16).astype(F32)
        message_ref[2 * QBLK : 2 * QBLK + 2 * share, :] = jnp.zeros((2 * share, width), BF16)
        message_ref[2 * QBLK : 2 * QBLK + 2 * share, 0:DH] = jnp.concatenate(
            [high, rows - high], axis=0
        ).astype(BF16)


def main_kernel(place_ref, lists_ref, lengths_ref, pass_dev, incoming_ref, *rest):
    parts = lists_ref.shape[0]
    message_refs = rest[:parts]
    dq_refs = rest[parts : 2 * parts]
    out_ref, k_ref, v_ref, bias_ref = rest[2 * parts :]
    list_len = lists_ref.shape[1]
    plen = incoming_ref.shape[1] // 2
    width = message_refs[0].shape[1]
    share = width // DH
    scale = DH ** (-0.5)
    out_ref[...] = jnp.zeros_like(out_ref)
    slot_row = lax.broadcasted_iota(jnp.int32, (plen, DH), 0)
    for j, (message_ref, dq_ref) in enumerate(zip(message_refs, dq_refs)):
        block = lax.rem(place_ref[0] + parts - j, parts)
        slots = []
        for p in range(list_len):
            passage = lists_ref[block, p]
            slot = slot_of(passage // pass_dev)
            slots.append(slot)
            rows = slice(p * plen, (p + 1) * plen)
            k_ref[rows, :] = incoming_ref[slot, 0:plen, :]
            v_ref[rows, :] = incoming_ref[slot, plen : 2 * plen, :]
            bias_ref[rows, :] = jnp.where(slot_row < lengths_ref[passage], 0.0, MASKED)
        keys = k_ref[...]
        values = v_ref[...]
        heads = [slice(h * DH, (h + 1) * DH) for h in range(share)]
        queries = jnp.concatenate([message_ref[0:QBLK, c] for c in heads], axis=0)
        grads = jnp.concatenate([message_ref[QBLK : 2 * QBLK, c] for c in heads], axis=0)
        delta_parts = message_ref[2 * QBLK : 2 * QBLK + 2 * share, 0:DH].astype(F32)
        delta = delta_parts[:share] + delta_parts[share:]
        delta = jnp.concatenate([delta[h : h + 1] for h in range(share)], axis=1)
        bias = jnp.concatenate([bias_ref[...]] * share, axis=1)
        scores = lax.dot_general(keys, queries, NT, preferred_element_type=F32) * scale + bias
        weights = jnp.exp(scores - jnp.max(scores, axis=0, keepdims=True))
        weights = weights * (1.0 / jnp.sum(weights, axis=0, keepdims=True))
        weight_grads = lax.dot_general(values, grads, NT, preferred_element_type=F32)
        score_grads = (weights * (weight_grads - delta)).astype(BF16)
        value_term = jnp.dot(weights.astype(BF16), grads, preferred_element_type=F32).astype(BF16)
        key_term = (jnp.dot(score_grads, queries, preferred_element_type=F32) * scale).astype(BF16)
        for p, slot in enumerate(slots):
            rows = slice(p * plen, (p + 1) * plen)
            out_ref[slot, 0:plen, :] = key_term[rows]
            out_ref[slot, plen : 2 * plen, :] = value_term[rows]
        query_part = lax.dot_general(keys, score_grads, TN, preferred_element_type=F32) * scale
        for c in heads:
            dq_ref[:, c] = query_part[:, c].T.astype(BF16)


def place_kernel(place_ref, *rest):
    *piece_refs, out_ref = rest
    parts = len(piece_refs)
    width = out_ref.shape[1] // parts
    for j, piece_ref in enumerate(piece_refs):
        to = lax.rem(place_ref[0] + j, parts)
        out_ref[:, pl.ds(pl.multiple_of(to * width, width), width)] = piece_ref[...]


def sum_kernel(pick_ref, terms_ref, keys_ref, values_ref):
    pass_dev, plen, _ = keys_ref.shape

    def body(n, sums):
        k = pick_ref[n]
        term = terms_ref[slot_of(n)].astype(F32)
        return tuple(s + jnp.where(k == i, term, 0.0) for i, s in enumerate(sums))

    zero = jnp.zeros((2 * plen, DH), F32)
    sums = lax.fori_loop(0, terms_ref.shape[0], body, (zero,) * pass_dev, unroll=8)
    for i, s in enumerate(sums):
        keys_ref[i] = s[:plen].astype(BF16)
        values_ref[i] = s[plen:].astype(BF16)


def local(queries, grad_out, attn_out, passage_keys, passage_values, block_lists, passage_lengths):
    shards = lax.axis_size(SHARD_AXES)
    parts = lax.axis_size("tensor")
    my_shard = lax.axis_index(SHARD_AXES)
    place = lax.axis_index("tensor").astype(jnp.int32).reshape(1)
    pass_dev, plen, _ = passage_keys.shape
    rows, columns = queries.shape
    width = columns // parts
    list_len = block_lists.shape[1]
    all_shape = jax.ShapeDtypeStruct((shards, 2 * plen, DH), BF16)

    picked = jnp.where(block_lists // pass_dev == my_shard, block_lists % pass_dev + 1, 0)
    pick = jnp.sum(picked.reshape(shards, parts * list_len), axis=1) - 1

    outgoing = pl.pallas_call(
        send_kernel,
        out_shape=all_shape,
        in_specs=[smem(), vmem(), vmem()],
        out_specs=vmem(),
        compiler_params=params(),
        name="send",
    )(pick, passage_keys, passage_values)
    incoming = exchange(outgoing)

    message = jax.ShapeDtypeStruct((2 * QBLK + 2 * (width // DH), width), BF16)
    messages = pl.pallas_call(
        prep_kernel,
        out_shape=[message] * parts,
        in_specs=[smem(), vmem(), vmem(), vmem()],
        out_specs=[vmem()] * parts,
        scratch_shapes=[pltpu.VMEM((DH, QBLK), F32)],
        compiler_params=params(),
        cost_estimate=pl.CostEstimate(flops=2 * rows * columns, bytes_accessed=10 * rows * columns, transcendentals=0),
        name="prep",
    )(place, queries, grad_out, attn_out)

    def shift(piece, by):
        if by == 0:
            return piece
        return lax.ppermute(piece, "tensor", [(i, (i + by) % parts) for i in range(parts)])

    messages = [shift(piece, j) for j, piece in enumerate(messages)]
    own_lists = lax.dynamic_slice_in_dim(block_lists, my_shard * parts, parts, 0)

    def main(place_ref, lists_ref, lengths_ref, *refs):
        main_kernel(place_ref, lists_ref, lengths_ref, pass_dev, *refs)

    keys = list_len * plen
    pairs = parts * QBLK * (width // DH) * keys
    *query_parts, outgoing_grads = pl.pallas_call(
        main,
        out_shape=[jax.ShapeDtypeStruct((QBLK, width), BF16)] * parts + [all_shape],
        in_specs=[smem(), smem(), smem(), vmem()] + [vmem()] * parts,
        out_specs=[vmem()] * (parts + 1),
        scratch_shapes=[
            pltpu.VMEM((keys, DH), BF16),
            pltpu.VMEM((keys, DH), BF16),
            pltpu.VMEM((keys, DH), F32),
        ],
        compiler_params=params(),
        cost_estimate=pl.CostEstimate(flops=10 * pairs * DH, bytes_accessed=8 * rows * columns, transcendentals=pairs),
        name="attention",
    )(place, own_lists, passage_lengths, incoming, *messages)

    returned = exchange(outgoing_grads)
    query_parts = [shift(piece, (parts - j) % parts) for j, piece in enumerate(query_parts)]
    query_grad = pl.pallas_call(
        place_kernel,
        out_shape=jax.ShapeDtypeStruct((rows, columns), BF16),
        in_specs=[smem()] + [vmem()] * parts,
        out_specs=vmem(),
        compiler_params=params(),
        cost_estimate=pl.CostEstimate(flops=0, bytes_accessed=4 * rows * columns, transcendentals=0),
        name="place",
    )(place, *query_parts)
    grad_shape = jax.ShapeDtypeStruct(passage_keys.shape, BF16)
    key_grad, value_grad = pl.pallas_call(
        sum_kernel,
        out_shape=[grad_shape, grad_shape],
        in_specs=[smem(), vmem()],
        out_specs=[vmem(), vmem()],
        compiler_params=params(),
        name="sum",
    )(pick, returned)
    return query_grad, key_grad, value_grad


def solution(mesh):
    parts = mesh.shape["tensor"]
    fine = Mesh(mesh.devices.reshape((2,) * len(SHARD_AXES) + (parts,)), SHARD_AXES + ("tensor",))
    tokens = P(SHARD_AXES + ("tensor",), None)
    passages = P(SHARD_AXES, None, "tensor")
    return jax.shard_map(
        local,
        mesh=fine,
        in_specs=(tokens, tokens, tokens, passages, passages, P(), P()),
        out_specs=(tokens, passages, passages),
        check_vma=False,
    )
```

```python
import jax
import jax.numpy as jnp
from jax import lax
from jax.experimental import pallas as pl
from jax.experimental.pallas import tpu as pltpu
from jax.sharding import Mesh
from jax.sharding import PartitionSpec as P

DH = 128
QBLK = 128
BF16 = jnp.bfloat16
F32 = jnp.float32
MASKED = -1e30
NT = (((1,), (1,)), ((), ()))
TN = (((0,), (0,)), ((), ()))
SMALL_VMEM = 24 * 1024 * 1024
LARGE_VMEM = 60 * 1024 * 1024


SHARD_AXES = ("y2", "y1", "y0", "z2", "z1", "z0", "core")
EXCHANGE_AXES = ("core", "y0", "z0", "y1", "z1", "y2", "z2")


def slot_of(shard):
    bits = len(SHARD_AXES)
    slot = 0
    for i, name in enumerate(EXCHANGE_AXES):
        bit = (shard >> (bits - 1 - SHARD_AXES.index(name))) & 1
        slot = slot | (bit << (bits - 1 - i))
    return slot


def exchange(pieces):
    return lax.all_to_all(pieces, EXCHANGE_AXES, split_axis=0, concat_axis=0, tiled=True)


def vmem():
    return pl.BlockSpec(memory_space=pltpu.VMEM)


def hbm():
    return pl.BlockSpec(memory_space=pltpu.HBM)


def smem():
    return pl.BlockSpec(memory_space=pltpu.SMEM)


def params(limit=SMALL_VMEM):
    return pltpu.CompilerParams(vmem_limit_bytes=limit)


def send_kernel(base_ref, lists_ref, keys_ref, values_ref, out_ref, pick_ref, row_ref, scalar_ref, built_ref, sems):
    pass_dev, plen, _ = keys_ref.shape
    shards = out_ref.shape[0]
    blocks = lists_ref.shape[1] // shards
    here = lists_ref[...] - base_ref[0]
    here = jnp.where((here >= 0) & (here < pass_dev), here + 1, 0)
    row_ref[...] = jnp.sum(here, axis=0, keepdims=True)
    copy = pltpu.make_async_copy(row_ref, scalar_ref, sems.at[0])
    copy.start()
    copy.wait()
    for n in range(shards):
        k = scalar_ref[0, n * blocks]
        for b in range(1, blocks):
            k = k + scalar_ref[0, n * blocks + b]
        k = k - 1
        pick_ref[n] = k
        k = jnp.maximum(k, 0)
        slot = slot_of(n)
        built_ref[slot, 0:plen, :] = keys_ref[k]
        built_ref[slot, plen : 2 * plen, :] = values_ref[k]
    copy = pltpu.make_async_copy(built_ref, out_ref, sems.at[1])
    copy.start()
    copy.wait()


def prep_kernel(place_ref, q_ref, g_ref, o_ref, message_ref, o_piece, sems):
    width = message_ref.shape[1]
    share = width // DH
    cols = pl.ds(pl.multiple_of(place_ref[0] * width, width), width)
    copies = [
        pltpu.make_async_copy(g_ref.at[:, cols], message_ref.at[QBLK : 2 * QBLK, :], sems.at[0]),
        pltpu.make_async_copy(o_ref.at[:, cols], o_piece, sems.at[1]),
        pltpu.make_async_copy(q_ref.at[:, cols], message_ref.at[0:QBLK, :], sems.at[2]),
    ]
    for copy in copies:
        copy.start()
    copies[0].wait()
    copies[1].wait()
    lane = lax.broadcasted_iota(jnp.int32, (QBLK, DH), 1)
    delta = jnp.zeros((QBLK, DH), F32)
    for h in range(share):
        c = slice(h * DH, (h + 1) * DH)
        term = message_ref[QBLK : 2 * QBLK, c].astype(F32) * o_piece[:, c].astype(F32)
        delta = jnp.where(lane == h, jnp.sum(term, axis=1, keepdims=True), delta)
    delta = delta.T[:share]
    high = delta.astype(BF16).astype(F32)
    message_ref[2 * QBLK :, :] = jnp.zeros((2 * share, width), BF16)
    message_ref[2 * QBLK :, 0:DH] = jnp.concatenate([high, delta - high], axis=0).astype(BF16)
    copies[2].wait()


def main_kernel(place_ref, slots_ref, lists_ref, lengths_ref, incoming_ref, *rest):
    parts, list_len = lists_ref.shape
    message_refs = rest[:parts]
    dq_refs = rest[parts : 2 * parts]
    out_ref, messages_ref, kv_ref, terms_ref, bias_ref, kv_sems, message_sems, out_sems = rest[2 * parts :]
    plen = incoming_ref.shape[1] // 2
    keys_here = list_len * plen
    share = message_refs[0].shape[1] // DH
    scale = DH ** (-0.5)
    slot_row = lax.broadcasted_iota(jnp.int32, (plen, DH), 0)
    blocks = [lax.rem(place_ref[0] + parts - j, parts) for j in range(parts)]
    slots = [[slots_ref[block, p] for p in range(list_len)] for block in blocks]
    loads = []
    for j in range(parts):
        copies = [pltpu.make_async_copy(message_refs[j], messages_ref.at[j], message_sems.at[j])]
        for p, slot in enumerate(slots[j]):
            copies.append(pltpu.make_async_copy(incoming_ref.at[slot], kv_ref.at[j, p], kv_sems.at[j, p]))
        for copy in copies:
            copy.start()
        loads.append(copies)
    stores = []
    for j, dq_ref in enumerate(dq_refs):
        message_ref = messages_ref.at[j]
        for p in range(list_len):
            rows = slice(p * plen, (p + 1) * plen)
            bias_ref[rows, :] = jnp.where(slot_row < lengths_ref[lists_ref[blocks[j], p]], 0.0, MASKED)
        for copy in loads[j]:
            copy.wait()
        keys = kv_ref[j, :, 0:plen, :].reshape(keys_here, DH)
        values = kv_ref[j, :, plen : 2 * plen, :].reshape(keys_here, DH)
        heads = [slice(h * DH, (h + 1) * DH) for h in range(share)]
        queries = jnp.concatenate([message_ref[0:QBLK, c] for c in heads], axis=0)
        grads = jnp.concatenate([message_ref[QBLK : 2 * QBLK, c] for c in heads], axis=0)
        delta_parts = message_ref[2 * QBLK : 2 * QBLK + 2 * share, 0:DH].astype(F32)
        delta = delta_parts[:share] + delta_parts[share:]
        delta = jnp.concatenate([delta[h : h + 1] for h in range(share)], axis=1)
        bias = jnp.concatenate([bias_ref[...]] * share, axis=1)
        scores = lax.dot_general(keys, queries, NT, preferred_element_type=F32) * scale + bias
        weights = jnp.exp(scores - jnp.max(scores, axis=0, keepdims=True))
        weights = weights * (1.0 / jnp.sum(weights, axis=0, keepdims=True))
        weight_grads = lax.dot_general(values, grads, NT, preferred_element_type=F32)
        score_grads = (weights * (weight_grads - delta)).astype(BF16)
        value_term = jnp.dot(weights.astype(BF16), grads, preferred_element_type=F32).astype(BF16)
        key_term = (jnp.dot(score_grads, queries, preferred_element_type=F32) * scale).astype(BF16)
        terms_ref[j, :, 0:plen, :] = key_term.reshape(list_len, plen, DH)
        terms_ref[j, :, plen : 2 * plen, :] = value_term.reshape(list_len, plen, DH)
        for p, slot in enumerate(slots[j]):
            copy = pltpu.make_async_copy(terms_ref.at[j, p], out_ref.at[slot], out_sems.at[j, p])
            copy.start()
            stores.append(copy)
        query_part = lax.dot_general(keys, score_grads, TN, preferred_element_type=F32) * scale
        for c in heads:
            dq_ref[:, c] = query_part[:, c].T.astype(BF16)
    for copy in stores:
        copy.wait()


def place_kernel(place_ref, *rest):
    *piece_refs, out_ref = rest
    parts = len(piece_refs)
    width = out_ref.shape[1] // parts
    for j, piece_ref in enumerate(piece_refs):
        to = lax.rem(place_ref[0] + j, parts)
        out_ref[:, pl.ds(pl.multiple_of(to * width, width), width)] = piece_ref[...]


def sum_kernel(pick_ref, terms_ref, keys_ref, values_ref):
    pass_dev, plen, _ = keys_ref.shape
    sums = [jnp.zeros((2 * plen, DH), F32)] * pass_dev
    for n in range(terms_ref.shape[0]):
        k = pick_ref[n]
        term = terms_ref[slot_of(n)].astype(F32)
        sums = [s + jnp.where(k == i, term, 0.0) for i, s in enumerate(sums)]
    for i, s in enumerate(sums):
        keys_ref[i] = s[:plen].astype(BF16)
        values_ref[i] = s[plen:].astype(BF16)


def local(queries, grad_out, attn_out, passage_keys, passage_values, block_lists, passage_lengths):
    shards = lax.axis_size(SHARD_AXES)
    parts = lax.axis_size("tensor")
    my_shard = lax.axis_index(SHARD_AXES)
    place = lax.axis_index("tensor").astype(jnp.int32).reshape(1)
    pass_dev, plen, _ = passage_keys.shape
    rows, columns = queries.shape
    width = columns // parts
    list_len = block_lists.shape[1]
    all_shape = jax.ShapeDtypeStruct((shards, 2 * plen, DH), BF16)

    share = width // DH
    message = jax.ShapeDtypeStruct((2 * QBLK + 2 * share, width), BF16)

    def prep(by):
        to = lax.rem(place + by, parts)
        return pl.pallas_call(
            prep_kernel,
            out_shape=message,
            in_specs=[smem(), hbm(), hbm(), hbm()],
            out_specs=vmem(),
            scratch_shapes=[pltpu.VMEM((QBLK, width), BF16), pltpu.SemaphoreType.DMA((3,))],
            compiler_params=params(LARGE_VMEM),
            cost_estimate=pl.CostEstimate(flops=2 * rows * width, bytes_accessed=10 * rows * width, transcendentals=0),
            name="prep",
        )(to, queries, grad_out, attn_out)

    def shift(piece, by):
        if by == 0:
            return piece
        return lax.ppermute(piece, "tensor", [(i, (i + by) % parts) for i in range(parts)])

    outgoing, pick = pl.pallas_call(
        send_kernel,
        out_shape=[all_shape, jax.ShapeDtypeStruct((shards,), jnp.int32)],
        in_specs=[smem(), vmem(), vmem(), vmem()],
        out_specs=[hbm(), smem()],
        scratch_shapes=[
            pltpu.VMEM((1, shards * parts), jnp.int32),
            pltpu.SMEM((1, shards * parts), jnp.int32),
            pltpu.VMEM(all_shape.shape, BF16),
            pltpu.SemaphoreType.DMA((2,)),
        ],
        compiler_params=params(LARGE_VMEM),
        name="send",
    )((my_shard * pass_dev).astype(jnp.int32).reshape(1), block_lists.T, passage_keys, passage_values)
    incoming = exchange(outgoing)
    messages = [shift(prep(j), j) for j in range(parts)]
    own_lists = lax.dynamic_slice_in_dim(block_lists, my_shard * parts, parts, 0)

    own_slots = slot_of(own_lists // pass_dev)
    keys = list_len * plen
    pairs = parts * QBLK * share * keys
    *query_parts, outgoing_grads = pl.pallas_call(
        main_kernel,
        out_shape=[jax.ShapeDtypeStruct((QBLK, width), BF16)] * parts + [all_shape],
        in_specs=[smem()] * 4 + [hbm()] + [pl.BlockSpec(memory_space=pl.ANY)] * parts,
        out_specs=[vmem()] * parts + [hbm()],
        scratch_shapes=[
            pltpu.VMEM((parts,) + message.shape, BF16),
            pltpu.VMEM((parts, list_len, 2 * plen, DH), BF16),
            pltpu.VMEM((parts, list_len, 2 * plen, DH), BF16),
            pltpu.VMEM((keys, DH), F32),
            pltpu.SemaphoreType.DMA((parts, list_len)),
            pltpu.SemaphoreType.DMA((parts,)),
            pltpu.SemaphoreType.DMA((parts, list_len)),
        ],
        compiler_params=params(),
        cost_estimate=pl.CostEstimate(flops=10 * pairs * DH, bytes_accessed=8 * rows * columns, transcendentals=pairs),
        name="attention",
    )(place, own_slots, own_lists, passage_lengths, incoming, *messages)

    returned = exchange(outgoing_grads)
    query_parts = [shift(piece, (parts - j) % parts) for j, piece in enumerate(query_parts)]
    query_grad = pl.pallas_call(
        place_kernel,
        out_shape=jax.ShapeDtypeStruct((rows, columns), BF16),
        in_specs=[smem()] + [vmem()] * parts,
        out_specs=vmem(),
        compiler_params=params(),
        cost_estimate=pl.CostEstimate(flops=0, bytes_accessed=4 * rows * columns, transcendentals=0),
        name="place",
    )(place, *query_parts)
    grad_shape = jax.ShapeDtypeStruct(passage_keys.shape, BF16)
    key_grad, value_grad = pl.pallas_call(
        sum_kernel,
        out_shape=[grad_shape, grad_shape],
        in_specs=[smem(), vmem()],
        out_specs=[vmem(), vmem()],
        compiler_params=params(),
        name="sum",
    )(pick, returned)
    return query_grad, key_grad, value_grad


def solution(mesh):
    parts = mesh.shape["tensor"]
    fine = Mesh(mesh.devices.reshape((2,) * len(SHARD_AXES) + (parts,)), SHARD_AXES + ("tensor",))
    tokens = P(SHARD_AXES + ("tensor",), None)
    passages = P(SHARD_AXES, None, "tensor")
    return jax.shard_map(
        local,
        mesh=fine,
        in_specs=(tokens, tokens, tokens, passages, passages, P(), P()),
        out_specs=(tokens, passages, passages),
        check_vma=False,
    )
```

```python
import jax
import jax.numpy as jnp
from jax import lax
from jax.experimental import pallas as pl
from jax.experimental.pallas import tpu as pltpu
from jax.sharding import Mesh
from jax.sharding import PartitionSpec as P

DH = 128
QBLK = 128
BF16 = jnp.bfloat16
F32 = jnp.float32
MASKED = -1e30
LOG2E = 1.4426950408889634
NT = (((1,), (1,)), ((), ()))
TN = (((0,), (0,)), ((), ()))
SMALL_VMEM = 24 * 1024 * 1024
LARGE_VMEM = 60 * 1024 * 1024


SHARD_AXES = ("y2", "y1", "y0", "z2", "z1", "z0", "core")
EXCHANGE_AXES = ("core", "y0", "z0", "y1", "z1", "y2", "z2")


def slot_of(shard):
    bits = len(SHARD_AXES)
    slot = 0
    for i, name in enumerate(EXCHANGE_AXES):
        bit = (shard >> (bits - 1 - SHARD_AXES.index(name))) & 1
        slot = slot | (bit << (bits - 1 - i))
    return slot


def exchange(pieces):
    return lax.all_to_all(pieces, EXCHANGE_AXES, split_axis=0, concat_axis=0, tiled=True)


def vmem():
    return pl.BlockSpec(memory_space=pltpu.VMEM)


def hbm():
    return pl.BlockSpec(memory_space=pltpu.HBM)


def smem():
    return pl.BlockSpec(memory_space=pltpu.SMEM)


def params(limit=SMALL_VMEM):
    return pltpu.CompilerParams(vmem_limit_bytes=limit)


def send_kernel(base_ref, lists_ref, keys_ref, values_ref, out_ref, pick_ref):
    pass_dev = keys_ref.shape[0]
    shards = out_ref.shape[0]
    blocks = lists_ref.shape[1] // shards
    here = lists_ref[...] - base_ref[0]
    here = jnp.where((here >= 0) & (here < pass_dev), here + 1, 0)
    here = jnp.sum(here, axis=0, keepdims=True)
    pick = here
    for b in range(1, blocks):
        pick = pick + pltpu.roll(here, here.shape[1] - b, 1)
    pick_ref[...] = pick
    tiles = [jnp.concatenate([keys_ref[i], values_ref[i]], axis=0) for i in range(pass_dev)]
    for n in range(shards):
        k = jnp.broadcast_to(pick[:, n * blocks : n * blocks + 1], tiles[0].shape)
        tile = tiles[0]
        for i in range(1, pass_dev):
            tile = jnp.where(k == i + 1, tiles[i], tile)
        out_ref[slot_of(n)] = tile


def prep_kernel(place_ref, q_ref, g_ref, o_ref, *rest):
    *message_refs, own_ref, delta_ref = rest
    parts = len(message_refs) + 1
    width = q_ref.shape[1] // parts
    share = width // DH
    lane = lax.broadcasted_iota(jnp.int32, (QBLK, DH), 1)
    delta = jnp.zeros((QBLK, DH), F32)
    for h in range(parts * share):
        cols = slice(h * DH, (h + 1) * DH)
        term = jnp.sum(g_ref[:, cols].astype(F32) * o_ref[:, cols].astype(F32), axis=1, keepdims=True)
        delta = jnp.where(lane == h, term, delta)
    delta_ref[...] = delta.T
    for j in range(parts):
        to = lax.rem(place_ref[0] + j, parts)
        rows = delta_ref[pl.ds(pl.multiple_of(to * share, share), share), :]
        high = rows.astype(BF16).astype(F32)
        rows = jnp.concatenate([high, rows - high], axis=0).astype(BF16)
        if j == 0:
            own_ref[...] = rows
            continue
        message_ref = message_refs[j - 1]
        cols = pl.ds(pl.multiple_of(to * width, width), width)
        message_ref[0:QBLK, :] = q_ref[:, cols]
        message_ref[QBLK : 2 * QBLK, :] = g_ref[:, cols]
        message_ref[2 * QBLK :, :] = jnp.zeros((2 * share, width), BF16)
        message_ref[2 * QBLK :, 0:DH] = rows


def main_kernel(place_ref, slots_ref, lists_ref, lengths_ref, incoming_ref, q_ref, g_ref, own_delta_ref, *rest):
    parts, list_len = lists_ref.shape
    message_refs = rest[: parts - 1]
    query_grad_ref, dq_ref, out_ref, own_ref, own_dq_ref, k_ref, v_ref, terms_ref, bias_ref, own_sems, out_sems = rest[parts - 1 :]
    plen = incoming_ref.shape[1] // 2
    width = own_ref.shape[1]
    share = width // DH
    scale = DH ** (-0.5)
    heads = [slice(h * DH, (h + 1) * DH) for h in range(share)]
    own_cols = pl.ds(pl.multiple_of(place_ref[0] * width, width), width)
    own_copies = [
        pltpu.make_async_copy(q_ref.at[:, own_cols], own_ref.at[0:QBLK, :], own_sems.at[0]),
        pltpu.make_async_copy(g_ref.at[:, own_cols], own_ref.at[QBLK : 2 * QBLK, :], own_sems.at[1]),
    ]
    for copy in own_copies:
        copy.start()
    slot_row = lax.broadcasted_iota(jnp.int32, (plen, DH), 0)
    rows_refs = list(message_refs) + [own_ref]
    delta_refs = [ref.at[2 * QBLK :, 0:DH] for ref in message_refs] + [own_delta_ref]
    result_refs = [dq_ref.at[j] for j in range(parts - 1)] + [own_dq_ref]
    all_slots = []
    for j in range(parts):
        block = lax.rem(place_ref[0] + parts - 1 - j, parts)
        all_slots.append([slots_ref[block, p] for p in range(list_len)])
        for p, slot in enumerate(all_slots[j]):
            rows = slice(p * plen, (p + 1) * plen)
            k_ref[j, rows, :] = incoming_ref[slot, 0:plen, :]
            v_ref[j, rows, :] = incoming_ref[slot, plen : 2 * plen, :]
            bias_ref[j, rows, :] = jnp.where(slot_row < lengths_ref[lists_ref[block, p]], 0.0, MASKED)

    def products(j):
        if j == parts - 1:
            for copy in own_copies:
                copy.wait()
        queries = jnp.concatenate([rows_refs[j][0:QBLK, c] for c in heads], axis=0)
        grads = jnp.concatenate([rows_refs[j][QBLK : 2 * QBLK, c] for c in heads], axis=0)
        scores = lax.dot_general(k_ref[j], queries, NT, preferred_element_type=F32)
        weight_grads = lax.dot_general(v_ref[j], grads, NT, preferred_element_type=F32)
        return queries, grads, scores, weight_grads

    stores = []
    ahead = products(0)
    for j in range(parts):
        queries, grads, scores, weight_grads = ahead
        if j + 1 < parts:
            ahead = products(j + 1)
        delta = delta_refs[j][...].astype(F32)
        delta = delta[:share] + delta[share:]
        delta = jnp.concatenate([delta[h : h + 1] for h in range(share)], axis=1)
        scores = scores * (scale * LOG2E) + jnp.concatenate([bias_ref[j]] * share, axis=1)
        weights = jnp.exp2(scores - jnp.max(scores, axis=0, keepdims=True))
        weights = weights * (1.0 / jnp.sum(weights, axis=0, keepdims=True))
        score_grads = (weights * (weight_grads - delta)).astype(BF16)
        value_term = jnp.dot(weights.astype(BF16), grads, preferred_element_type=F32)
        key_term = jnp.dot(score_grads, queries, preferred_element_type=F32) * scale
        terms_ref[j, :, 0:plen, :] = key_term.astype(BF16).reshape(list_len, plen, DH)
        terms_ref[j, :, plen : 2 * plen, :] = value_term.astype(BF16).reshape(list_len, plen, DH)
        for p, slot in enumerate(all_slots[j]):
            copy = pltpu.make_async_copy(terms_ref.at[j, p], out_ref.at[slot], out_sems.at[j, p])
            copy.start()
            stores.append(copy)
        query_part = lax.dot_general(k_ref[j], score_grads, TN, preferred_element_type=F32) * scale
        for c in heads:
            result_refs[j][:, c] = query_part[:, c].T.astype(BF16)
    copy = pltpu.make_async_copy(own_dq_ref, query_grad_ref.at[:, own_cols], own_sems.at[0])
    copy.start()
    stores.append(copy)
    for copy in stores:
        copy.wait()


def place_kernel(place_ref, own_ref, *rest):
    del own_ref
    *piece_refs, out_ref, sems = rest
    parts = len(piece_refs) + 1
    width = out_ref.shape[1] // parts
    copies = []
    for j, piece_ref in enumerate(piece_refs):
        to = lax.rem(place_ref[0] + j + 1, parts)
        cols = pl.ds(pl.multiple_of(to * width, width), width)
        copies.append(pltpu.make_async_copy(piece_ref, out_ref.at[:, cols], sems.at[j]))
    for copy in copies:
        copy.start()
    for copy in copies:
        copy.wait()


def sum_kernel(pick_ref, terms_ref, keys_ref, values_ref, total_ref):
    pass_dev, plen, _ = keys_ref.shape
    shards = terms_ref.shape[0]
    blocks = pick_ref.shape[1] // shards
    ways = total_ref.shape[0]
    total_ref[...] = jnp.zeros_like(total_ref)
    for n in range(shards):
        total_ref[n % ways, pick_ref[0, n * blocks]] += terms_ref[slot_of(n)].astype(F32)
    for i in range(pass_dev):
        total = total_ref[0, i + 1]
        for w in range(1, ways):
            total = total + total_ref[w, i + 1]
        keys_ref[i] = total[:plen].astype(BF16)
        values_ref[i] = total[plen:].astype(BF16)


def local(queries, grad_out, attn_out, passage_keys, passage_values, block_lists, passage_lengths):
    shards = lax.axis_size(SHARD_AXES)
    parts = lax.axis_size("tensor")
    my_shard = lax.axis_index(SHARD_AXES)
    place = lax.axis_index("tensor").astype(jnp.int32).reshape(1)
    pass_dev, plen, _ = passage_keys.shape
    rows, columns = queries.shape
    width = columns // parts
    list_len = block_lists.shape[1]
    all_shape = jax.ShapeDtypeStruct((shards, 2 * plen, DH), BF16)

    share = width // DH
    message = jax.ShapeDtypeStruct((2 * QBLK + 2 * share, width), BF16)
    own_shape = jax.ShapeDtypeStruct((2 * share, QBLK), BF16)
    *messages, own_delta = pl.pallas_call(
        prep_kernel,
        out_shape=[message] * (parts - 1) + [own_shape],
        in_specs=[smem(), vmem(), vmem(), vmem()],
        out_specs=[vmem()] * parts,
        scratch_shapes=[pltpu.VMEM((DH, QBLK), F32)],
        compiler_params=params(),
        cost_estimate=pl.CostEstimate(flops=2 * rows * columns, bytes_accessed=10 * rows * columns, transcendentals=0),
        name="prep",
    )(place, queries, grad_out, attn_out)

    def shift(piece, by):
        if by == 0:
            return piece
        return lax.ppermute(piece, "tensor", [(i, (i + by) % parts) for i in range(parts)])

    base = (my_shard * pass_dev).astype(jnp.int32).reshape(1)
    outgoing, pick = pl.pallas_call(
        send_kernel,
        out_shape=[all_shape, jax.ShapeDtypeStruct((1, shards * parts), jnp.int32)],
        in_specs=[smem(), vmem(), vmem(), vmem()],
        out_specs=[vmem(), vmem()],
        compiler_params=params(LARGE_VMEM),
        name="send",
    )(base, block_lists.T, passage_keys, passage_values)
    incoming = exchange(outgoing)
    messages = [shift(piece, j + 1) for j, piece in enumerate(messages)]
    own_lists = lax.dynamic_slice_in_dim(block_lists, my_shard * parts, parts, 0)

    own_slots = slot_of(own_lists // pass_dev)
    keys = list_len * plen
    pairs = parts * QBLK * share * keys
    any_place = pl.BlockSpec(memory_space=pl.ANY)
    full_shape = jax.ShapeDtypeStruct((rows, columns), BF16)
    query_grad, query_parts, outgoing_grads = pl.pallas_call(
        main_kernel,
        out_shape=[full_shape, jax.ShapeDtypeStruct((parts - 1, QBLK, width), BF16), all_shape],
        in_specs=[smem()] * 4 + [vmem()] + [any_place] * 2 + [vmem()] * parts,
        out_specs=[hbm(), vmem(), hbm()],
        scratch_shapes=[
            pltpu.VMEM((2 * QBLK, width), BF16),
            pltpu.VMEM((QBLK, width), BF16),
            pltpu.VMEM((parts, keys, DH), BF16),
            pltpu.VMEM((parts, keys, DH), BF16),
            pltpu.VMEM((parts, list_len, 2 * plen, DH), BF16),
            pltpu.VMEM((parts, keys, DH), F32),
            pltpu.SemaphoreType.DMA((2,)),
            pltpu.SemaphoreType.DMA((parts, list_len)),
        ],
        compiler_params=params(),
        cost_estimate=pl.CostEstimate(flops=10 * pairs * DH, bytes_accessed=8 * rows * columns, transcendentals=pairs),
        name="attention",
    )(place, own_slots, own_lists, passage_lengths, incoming, queries, grad_out, own_delta, *messages)

    returned = exchange(outgoing_grads)
    query_parts = [shift(query_parts[j], parts - 1 - j) for j in range(parts - 1)]
    query_grad = pl.pallas_call(
        place_kernel,
        out_shape=full_shape,
        in_specs=[smem(), hbm()] + [vmem()] * (parts - 1),
        out_specs=hbm(),
        scratch_shapes=[pltpu.SemaphoreType.DMA((parts - 1,))],
        input_output_aliases={1: 0},
        compiler_params=params(),
        cost_estimate=pl.CostEstimate(flops=0, bytes_accessed=4 * rows * columns, transcendentals=0),
        name="place",
    )(place, query_grad, *query_parts)
    grad_shape = jax.ShapeDtypeStruct(passage_keys.shape, BF16)
    key_grad, value_grad = pl.pallas_call(
        sum_kernel,
        out_shape=[grad_shape, grad_shape],
        in_specs=[smem(), vmem()],
        out_specs=[vmem(), vmem()],
        scratch_shapes=[pltpu.VMEM((4, pass_dev + 1, 2 * plen, DH), F32)],
        compiler_params=params(),
        name="sum",
    )(pick, returned)
    return query_grad, key_grad, value_grad


def solution(mesh):
    parts = mesh.shape["tensor"]
    fine = Mesh(mesh.devices.reshape((2,) * len(SHARD_AXES) + (parts,)), SHARD_AXES + ("tensor",))
    tokens = P(SHARD_AXES + ("tensor",), None)
    passages = P(SHARD_AXES, None, "tensor")
    return jax.shard_map(
        local,
        mesh=fine,
        in_specs=(tokens, tokens, tokens, passages, passages, P(), P()),
        out_specs=(tokens, passages, passages),
        check_vma=False,
    )
```

```python
import jax
import jax.numpy as jnp
from jax import lax
from jax.experimental import pallas as pl
from jax.experimental.pallas import tpu as pltpu
from jax.sharding import Mesh
from jax.sharding import PartitionSpec as P

DH = 128
QBLK = 128
BF16 = jnp.bfloat16
F32 = jnp.float32
MASKED = -1e30
LOG2E = 1.4426950408889634
NT = (((1,), (1,)), ((), ()))
TN = (((0,), (0,)), ((), ()))
SMALL_VMEM = 24 * 1024 * 1024
LARGE_VMEM = 60 * 1024 * 1024


SHARD_AXES = ("y2", "y1", "y0", "z2", "z1", "z0", "core")
EXCHANGE_AXES = ("core", "y0", "z0", "y1", "z1", "y2", "z2")


def slot_of(shard):
    bits = len(SHARD_AXES)
    slot = 0
    for i, name in enumerate(EXCHANGE_AXES):
        bit = (shard >> (bits - 1 - SHARD_AXES.index(name))) & 1
        slot = slot | (bit << (bits - 1 - i))
    return slot


def exchange(pieces):
    return lax.all_to_all(pieces, EXCHANGE_AXES, split_axis=0, concat_axis=0, tiled=True)


def shifts(parts):
    far = parts // 2
    return (far,) + tuple(by for by in range(1, parts) if by != far)


def vmem():
    return pl.BlockSpec(memory_space=pltpu.VMEM)


def in_hbm(array):
    return pltpu.with_memory_space_constraint(array, pltpu.HBM)


def hbm():
    return pl.BlockSpec(memory_space=pltpu.HBM)


def smem():
    return pl.BlockSpec(memory_space=pltpu.SMEM)


def params(limit=SMALL_VMEM):
    return pltpu.CompilerParams(vmem_limit_bytes=limit)


def send_kernel(base_ref, lists_ref, keys_ref, values_ref, out_ref, pick_ref):
    pass_dev = keys_ref.shape[0]
    shards = out_ref.shape[0]
    blocks = lists_ref.shape[1] // shards
    here = lists_ref[...] - base_ref[0]
    here = jnp.where((here >= 0) & (here < pass_dev), here + 1, 0)
    here = jnp.sum(here, axis=0, keepdims=True)
    pick = here
    for b in range(1, blocks):
        pick = pick + pltpu.roll(here, here.shape[1] - b, 1)
    pick_ref[...] = pick
    tiles = [jnp.concatenate([keys_ref[i], values_ref[i]], axis=0) for i in range(pass_dev)]
    for n in range(shards):
        k = jnp.broadcast_to(pick[:, n * blocks : n * blocks + 1], tiles[0].shape)
        tile = tiles[0]
        for i in range(1, pass_dev):
            tile = jnp.where(k == i + 1, tiles[i], tile)
        out_ref[slot_of(n)] = tile


def prep_kernel(place_ref, q_ref, g_ref, o_ref, *rest):
    *message_refs, own_ref, delta_ref = rest
    parts = len(message_refs) + 1
    width = q_ref.shape[1] // parts
    share = width // DH
    lane = lax.broadcasted_iota(jnp.int32, (QBLK, DH), 1)
    delta = jnp.zeros((QBLK, DH), F32)
    for h in range(parts * share):
        cols = slice(h * DH, (h + 1) * DH)
        term = jnp.sum(g_ref[:, cols].astype(F32) * o_ref[:, cols].astype(F32), axis=1, keepdims=True)
        delta = jnp.where(lane == h, term, delta)
    delta_ref[...] = delta.T
    for j in range(parts):
        to = lax.rem(place_ref[0] + (0 if j == 0 else shifts(parts)[j - 1]), parts)
        rows = delta_ref[pl.ds(pl.multiple_of(to * share, share), share), :]
        high = rows.astype(BF16).astype(F32)
        rows = jnp.concatenate([high, rows - high], axis=0).astype(BF16)
        if j == 0:
            own_ref[...] = rows
            continue
        message_ref = message_refs[j - 1]
        cols = pl.ds(pl.multiple_of(to * width, width), width)
        message_ref[0:QBLK, :] = q_ref[:, cols]
        message_ref[QBLK : 2 * QBLK, :] = g_ref[:, cols]
        message_ref[2 * QBLK :, :] = jnp.zeros((2 * share, width), BF16)
        message_ref[2 * QBLK :, 0:DH] = rows


def main_kernel(place_ref, slots_ref, lists_ref, lengths_ref, incoming_ref, q_ref, g_ref, own_delta_ref, *rest):
    parts, list_len = lists_ref.shape
    message_refs = rest[: parts - 1]
    query_grad_ref, dq_ref, out_ref, own_ref, held_ref, own_dq_ref, k_ref, v_ref, terms_ref, bias_ref, own_sems, held_sems, out_sems = rest[parts - 1 :]
    plen = incoming_ref.shape[1] // 2
    width = own_ref.shape[1]
    share = width // DH
    scale = DH ** (-0.5)
    heads = [slice(h * DH, (h + 1) * DH) for h in range(share)]
    own_cols = pl.ds(pl.multiple_of(place_ref[0] * width, width), width)
    distances = (0,) + shifts(parts)
    loads = [
        [
            pltpu.make_async_copy(q_ref.at[:, own_cols], own_ref.at[0:QBLK, :], own_sems.at[0]),
            pltpu.make_async_copy(g_ref.at[:, own_cols], own_ref.at[QBLK : 2 * QBLK, :], own_sems.at[1]),
        ]
    ]
    for i, message_ref in enumerate(message_refs):
        loads.append([pltpu.make_async_copy(message_ref, held_ref.at[i], held_sems.at[i])])
    for copies in loads:
        for copy in copies:
            copy.start()
    slot_row = lax.broadcasted_iota(jnp.int32, (plen, DH), 0)
    rows_refs = [own_ref] + [held_ref.at[i] for i in range(parts - 1)]
    delta_refs = [own_delta_ref] + [held_ref.at[i, 2 * QBLK :, 0:DH] for i in range(parts - 1)]
    result_refs = [own_dq_ref] + [dq_ref.at[i] for i in range(parts - 1)]
    all_slots = []
    for j in range(parts):
        block = lax.rem(place_ref[0] + parts - distances[j], parts)
        all_slots.append([slots_ref[block, p] for p in range(list_len)])
        for p, slot in enumerate(all_slots[j]):
            rows = slice(p * plen, (p + 1) * plen)
            k_ref[j, rows, :] = incoming_ref[slot, 0:plen, :]
            v_ref[j, rows, :] = incoming_ref[slot, plen : 2 * plen, :]
            bias_ref[j, rows, :] = jnp.where(slot_row < lengths_ref[lists_ref[block, p]], 0.0, MASKED)

    def products(j):
        for copy in loads[j]:
            copy.wait()
        queries = jnp.concatenate([rows_refs[j][0:QBLK, c] for c in heads], axis=0)
        grads = jnp.concatenate([rows_refs[j][QBLK : 2 * QBLK, c] for c in heads], axis=0)
        scores = lax.dot_general(k_ref[j], queries, NT, preferred_element_type=F32)
        weight_grads = lax.dot_general(v_ref[j], grads, NT, preferred_element_type=F32)
        return queries, grads, scores, weight_grads

    stores = []
    ahead = products(0)
    for j in range(parts):
        queries, grads, scores, weight_grads = ahead
        if j + 1 < parts:
            ahead = products(j + 1)
        delta = delta_refs[j][...].astype(F32)
        delta = delta[:share] + delta[share:]
        delta = jnp.concatenate([delta[h : h + 1] for h in range(share)], axis=1)
        scores = scores * (scale * LOG2E) + jnp.concatenate([bias_ref[j]] * share, axis=1)
        weights = jnp.exp2(scores - jnp.max(scores, axis=0, keepdims=True))
        weights = weights * (1.0 / jnp.sum(weights, axis=0, keepdims=True))
        score_grads = (weights * (weight_grads - delta)).astype(BF16)
        value_term = jnp.dot(weights.astype(BF16), grads, preferred_element_type=F32)
        key_term = jnp.dot(score_grads, queries, preferred_element_type=F32) * scale
        terms_ref[j, :, 0:plen, :] = key_term.astype(BF16).reshape(list_len, plen, DH)
        terms_ref[j, :, plen : 2 * plen, :] = value_term.astype(BF16).reshape(list_len, plen, DH)
        for p, slot in enumerate(all_slots[j]):
            copy = pltpu.make_async_copy(terms_ref.at[j, p], out_ref.at[slot], out_sems.at[j, p])
            copy.start()
            stores.append(copy)
        query_part = lax.dot_general(k_ref[j], score_grads, TN, preferred_element_type=F32) * scale
        for c in heads:
            result_refs[j][:, c] = query_part[:, c].T.astype(BF16)
        if j == 0:
            copy = pltpu.make_async_copy(own_dq_ref, query_grad_ref.at[:, own_cols], own_sems.at[0])
            copy.start()
            stores.append(copy)
    for copy in stores:
        copy.wait()


def place_kernel(place_ref, own_ref, *rest):
    del own_ref
    *piece_refs, out_ref, sems = rest
    parts = len(piece_refs) + 1
    width = out_ref.shape[1] // parts
    copies = []
    for j, piece_ref in enumerate(piece_refs):
        to = lax.rem(place_ref[0] + shifts(parts)[j], parts)
        cols = pl.ds(pl.multiple_of(to * width, width), width)
        copies.append(pltpu.make_async_copy(piece_ref, out_ref.at[:, cols], sems.at[j]))
    for copy in copies:
        copy.start()
    for copy in copies:
        copy.wait()


def sum_kernel(pick_ref, terms_ref, keys_ref, values_ref, total_ref):
    pass_dev, plen, _ = keys_ref.shape
    shards = terms_ref.shape[0]
    blocks = pick_ref.shape[1] // shards
    ways = total_ref.shape[0]
    total_ref[...] = jnp.zeros_like(total_ref)
    for n in range(shards):
        total_ref[n % ways, pick_ref[0, n * blocks]] += terms_ref[slot_of(n)].astype(F32)
    for i in range(pass_dev):
        total = total_ref[0, i + 1]
        for w in range(1, ways):
            total = total + total_ref[w, i + 1]
        keys_ref[i] = total[:plen].astype(BF16)
        values_ref[i] = total[plen:].astype(BF16)


def local(queries, grad_out, attn_out, passage_keys, passage_values, block_lists, passage_lengths):
    shards = lax.axis_size(SHARD_AXES)
    parts = lax.axis_size("tensor")
    my_shard = lax.axis_index(SHARD_AXES)
    place = lax.axis_index("tensor").astype(jnp.int32).reshape(1)
    pass_dev, plen, _ = passage_keys.shape
    rows, columns = queries.shape
    width = columns // parts
    list_len = block_lists.shape[1]
    all_shape = jax.ShapeDtypeStruct((shards, 2 * plen, DH), BF16)

    share = width // DH
    message = jax.ShapeDtypeStruct((2 * QBLK + 2 * share, width), BF16)
    own_shape = jax.ShapeDtypeStruct((2 * share, QBLK), BF16)
    *messages, own_delta = pl.pallas_call(
        prep_kernel,
        out_shape=[message] * (parts - 1) + [own_shape],
        in_specs=[smem(), vmem(), vmem(), vmem()],
        out_specs=[vmem()] * parts,
        scratch_shapes=[pltpu.VMEM((DH, QBLK), F32)],
        compiler_params=params(),
        cost_estimate=pl.CostEstimate(flops=2 * rows * columns, bytes_accessed=10 * rows * columns, transcendentals=0),
        name="prep",
    )(place, queries, grad_out, attn_out)

    def shift(piece, by):
        if by == 0:
            return piece
        return lax.ppermute(piece, "tensor", [(i, (i + by) % parts) for i in range(parts)])

    base = (my_shard * pass_dev).astype(jnp.int32).reshape(1)
    outgoing, pick = pl.pallas_call(
        send_kernel,
        out_shape=[all_shape, jax.ShapeDtypeStruct((1, shards * parts), jnp.int32)],
        in_specs=[smem(), vmem(), vmem(), vmem()],
        out_specs=[vmem(), vmem()],
        compiler_params=params(LARGE_VMEM),
        name="send",
    )(base, block_lists.T, passage_keys, passage_values)
    incoming = exchange(outgoing)
    messages = [shift(piece, by) for piece, by in zip(messages, shifts(parts))]
    own_lists = lax.dynamic_slice_in_dim(block_lists, my_shard * parts, parts, 0)

    own_slots = slot_of(own_lists // pass_dev)
    keys = list_len * plen
    pairs = parts * QBLK * share * keys
    full_shape = jax.ShapeDtypeStruct((rows, columns), BF16)
    query_grad, query_parts, outgoing_grads = pl.pallas_call(
        main_kernel,
        out_shape=[full_shape, jax.ShapeDtypeStruct((parts - 1, QBLK, width), BF16), all_shape],
        in_specs=[smem()] * 4 + [vmem(), hbm(), hbm(), vmem()] + [hbm()] * (parts - 1),
        out_specs=[hbm(), vmem(), hbm()],
        scratch_shapes=[
            pltpu.VMEM((2 * QBLK, width), BF16),
            pltpu.VMEM((parts - 1,) + message.shape, BF16),
            pltpu.VMEM((QBLK, width), BF16),
            pltpu.VMEM((parts, keys, DH), BF16),
            pltpu.VMEM((parts, keys, DH), BF16),
            pltpu.VMEM((parts, list_len, 2 * plen, DH), BF16),
            pltpu.VMEM((parts, keys, DH), F32),
            pltpu.SemaphoreType.DMA((2,)),
            pltpu.SemaphoreType.DMA((parts - 1,)),
            pltpu.SemaphoreType.DMA((parts, list_len)),
        ],
        compiler_params=params(),
        cost_estimate=pl.CostEstimate(flops=10 * pairs * DH, bytes_accessed=8 * rows * columns, transcendentals=pairs),
        name="attention",
    )(place, own_slots, own_lists, passage_lengths, incoming, in_hbm(queries), in_hbm(grad_out), own_delta, *[in_hbm(piece) for piece in messages])

    returned = exchange(outgoing_grads)
    query_parts = [shift(query_parts[j], parts - by) for j, by in enumerate(shifts(parts))]
    query_grad = pl.pallas_call(
        place_kernel,
        out_shape=full_shape,
        in_specs=[smem(), hbm()] + [vmem()] * (parts - 1),
        out_specs=hbm(),
        scratch_shapes=[pltpu.SemaphoreType.DMA((parts - 1,))],
        input_output_aliases={1: 0},
        compiler_params=params(),
        cost_estimate=pl.CostEstimate(flops=0, bytes_accessed=4 * rows * columns, transcendentals=0),
        name="place",
    )(place, query_grad, *query_parts)
    grad_shape = jax.ShapeDtypeStruct(passage_keys.shape, BF16)
    key_grad, value_grad = pl.pallas_call(
        sum_kernel,
        out_shape=[grad_shape, grad_shape],
        in_specs=[smem(), vmem()],
        out_specs=[vmem(), vmem()],
        scratch_shapes=[pltpu.VMEM((4, pass_dev + 1, 2 * plen, DH), F32)],
        compiler_params=params(),
        name="sum",
    )(pick, returned)
    return query_grad, key_grad, value_grad


def solution(mesh):
    parts = mesh.shape["tensor"]
    fine = Mesh(mesh.devices.reshape((2,) * len(SHARD_AXES) + (parts,)), SHARD_AXES + ("tensor",))
    tokens = P(SHARD_AXES + ("tensor",), None)
    passages = P(SHARD_AXES, None, "tensor")
    return jax.shard_map(
        local,
        mesh=fine,
        in_specs=(tokens, tokens, tokens, passages, passages, P(), P()),
        out_specs=(tokens, passages, passages),
        check_vma=False,
    )
```

```python
import jax
import jax.numpy as jnp
from jax import lax
from jax.experimental import pallas as pl
from jax.experimental.pallas import tpu as pltpu
from jax.sharding import Mesh
from jax.sharding import PartitionSpec as P

DH = 128
QBLK = 128
BF16 = jnp.bfloat16
F32 = jnp.float32
MASKED = -1e30
LOG2E = 1.4426950408889634
NT = (((1,), (1,)), ((), ()))
TN = (((0,), (0,)), ((), ()))
SMALL_VMEM = 24 * 1024 * 1024
LARGE_VMEM = 60 * 1024 * 1024


SHARD_AXES = ("y2", "y1", "y0", "z2", "z1", "z0", "core")
EXCHANGE_AXES = ("core", "y0", "z0", "y1", "z1", "y2", "z2")


def slot_of(shard):
    bits = len(SHARD_AXES)
    slot = 0
    for i, name in enumerate(EXCHANGE_AXES):
        bit = (shard >> (bits - 1 - SHARD_AXES.index(name))) & 1
        slot = slot | (bit << (bits - 1 - i))
    return slot


def exchange(pieces):
    return lax.all_to_all(pieces, EXCHANGE_AXES, split_axis=0, concat_axis=0, tiled=True)


def shifts(parts):
    far = parts // 2
    return (far,) + tuple(by for by in range(1, parts) if by != far)


def vmem():
    return pl.BlockSpec(memory_space=pltpu.VMEM)


def in_hbm(array):
    return pltpu.with_memory_space_constraint(array, pltpu.HBM)


def hbm():
    return pl.BlockSpec(memory_space=pltpu.HBM)


def smem():
    return pl.BlockSpec(memory_space=pltpu.SMEM)


def params(limit=SMALL_VMEM):
    return pltpu.CompilerParams(vmem_limit_bytes=limit)


def send_kernel(base_ref, lists_ref, keys_ref, values_ref, out_ref, pick_ref):
    pass_dev = keys_ref.shape[0]
    shards = out_ref.shape[0]
    blocks = lists_ref.shape[1] // shards
    here = lists_ref[...] - base_ref[0]
    here = jnp.where((here >= 0) & (here < pass_dev), here + 1, 0)
    here = jnp.sum(here, axis=0, keepdims=True)
    pick = here
    for b in range(1, blocks):
        pick = pick + pltpu.roll(here, here.shape[1] - b, 1)
    pick_ref[...] = pick
    tiles = [jnp.concatenate([keys_ref[i], values_ref[i]], axis=0) for i in range(pass_dev)]
    for n in range(shards):
        k = jnp.broadcast_to(pick[:, n * blocks : n * blocks + 1], tiles[0].shape)
        tile = tiles[0]
        for i in range(1, pass_dev):
            tile = jnp.where(k == i + 1, tiles[i], tile)
        out_ref[slot_of(n)] = tile


def prep_kernel(place_ref, q_ref, g_ref, o_ref, *rest):
    *message_refs, own_ref, delta_ref = rest
    parts = len(message_refs) + 1
    width = q_ref.shape[1] // parts
    share = width // DH
    lane = lax.broadcasted_iota(jnp.int32, (QBLK, DH), 1)
    delta = jnp.zeros((QBLK, DH), F32)
    for h in range(parts * share):
        cols = slice(h * DH, (h + 1) * DH)
        term = jnp.sum(g_ref[:, cols].astype(F32) * o_ref[:, cols].astype(F32), axis=1, keepdims=True)
        delta = jnp.where(lane == h, term, delta)
    delta_ref[...] = delta.T
    for j in range(parts):
        to = lax.rem(place_ref[0] + (0 if j == 0 else shifts(parts)[j - 1]), parts)
        rows = delta_ref[pl.ds(pl.multiple_of(to * share, share), share), :]
        high = rows.astype(BF16).astype(F32)
        rows = jnp.concatenate([high, rows - high], axis=0).astype(BF16)
        if j == 0:
            own_ref[...] = rows
            continue
        message_ref = message_refs[j - 1]
        cols = pl.ds(pl.multiple_of(to * width, width), width)
        message_ref[0:QBLK, :] = q_ref[:, cols]
        message_ref[QBLK : 2 * QBLK, :] = g_ref[:, cols]
        message_ref[2 * QBLK :, :] = jnp.zeros((2 * share, width), BF16)
        message_ref[2 * QBLK :, 0:DH] = rows


def attend(slots_ref, lists_ref, lengths_ref, incoming_ref, blocks, pieces, out_ref, k_ref, v_ref, terms_ref, bias_ref, sems):
    list_len = lists_ref.shape[1]
    plen = incoming_ref.shape[1] // 2
    share = pieces[0][0].shape[1] // DH
    scale = DH ** (-0.5)
    heads = [slice(h * DH, (h + 1) * DH) for h in range(share)]
    slot_row = lax.broadcasted_iota(jnp.int32, (plen, DH), 0)
    all_slots = []
    for j, block in enumerate(blocks):
        all_slots.append([slots_ref[block, p] for p in range(list_len)])
        for p, slot in enumerate(all_slots[j]):
            rows = slice(p * plen, (p + 1) * plen)
            k_ref[j, rows, :] = incoming_ref[slot, 0:plen, :]
            v_ref[j, rows, :] = incoming_ref[slot, plen : 2 * plen, :]
            bias_ref[j, rows, :] = jnp.where(slot_row < lengths_ref[lists_ref[block, p]], 0.0, MASKED)

    def products(j):
        rows_ref, _, _, loads = pieces[j]
        for copy in loads:
            copy.wait()
        queries = jnp.concatenate([rows_ref[0:QBLK, c] for c in heads], axis=0)
        grads = jnp.concatenate([rows_ref[QBLK : 2 * QBLK, c] for c in heads], axis=0)
        scores = lax.dot_general(k_ref[j], queries, NT, preferred_element_type=F32)
        weight_grads = lax.dot_general(v_ref[j], grads, NT, preferred_element_type=F32)
        return queries, grads, scores, weight_grads

    stores = []
    ahead = products(0)
    for j in range(len(blocks)):
        queries, grads, scores, weight_grads = ahead
        if j + 1 < len(blocks):
            ahead = products(j + 1)
        _, delta_ref, result_ref, _ = pieces[j]
        delta = delta_ref[...].astype(F32)
        delta = delta[:share] + delta[share:]
        delta = jnp.concatenate([delta[h : h + 1] for h in range(share)], axis=1)
        scores = scores * (scale * LOG2E) + jnp.concatenate([bias_ref[j]] * share, axis=1)
        weights = jnp.exp2(scores - jnp.max(scores, axis=0, keepdims=True))
        weights = weights * (1.0 / jnp.sum(weights, axis=0, keepdims=True))
        score_grads = (weights * (weight_grads - delta)).astype(BF16)
        value_term = jnp.dot(weights.astype(BF16), grads, preferred_element_type=F32)
        key_term = jnp.dot(score_grads, queries, preferred_element_type=F32) * scale
        terms_ref[j, :, 0:plen, :] = key_term.astype(BF16).reshape(list_len, plen, DH)
        terms_ref[j, :, plen : 2 * plen, :] = value_term.astype(BF16).reshape(list_len, plen, DH)
        for p, slot in enumerate(all_slots[j]):
            copy = pltpu.make_async_copy(terms_ref.at[j, p], out_ref.at[slot], sems.at[j, p])
            copy.start()
            stores.append(copy)
        query_part = lax.dot_general(k_ref[j], score_grads, TN, preferred_element_type=F32) * scale
        for c in heads:
            result_ref[:, c] = query_part[:, c].T.astype(BF16)
    return stores


def first_kernel(place_ref, slots_ref, lists_ref, lengths_ref, incoming_ref, q_ref, g_ref, own_delta_ref, *rest):
    held = len(rest) - 13
    message_refs = rest[:held]
    query_grad_ref, dq_ref, out_ref, own_ref, held_ref, own_dq_ref = rest[held : held + 6]
    own_sems, held_sems = rest[held + 6 : held + 8]
    scratch = rest[held + 8 :]
    parts = lists_ref.shape[0]
    share = own_ref.shape[1] // DH
    width = own_ref.shape[1]
    own_cols = pl.ds(pl.multiple_of(place_ref[0] * width, width), width)
    loads = [
        pltpu.make_async_copy(q_ref.at[:, own_cols], own_ref.at[0:QBLK, :], own_sems.at[0]),
        pltpu.make_async_copy(g_ref.at[:, own_cols], own_ref.at[QBLK : 2 * QBLK, :], own_sems.at[1]),
    ]
    blocks = [place_ref[0]]
    pieces = [(own_ref, own_delta_ref, own_dq_ref, loads)]
    for i, message_ref in enumerate(message_refs):
        load = pltpu.make_async_copy(message_ref, held_ref.at[i], held_sems.at[i])
        blocks.append(lax.rem(place_ref[0] + parts - shifts(parts)[i], parts))
        pieces.append((held_ref.at[i], held_ref.at[i, 2 * QBLK : 2 * QBLK + 2 * share, 0:DH], dq_ref.at[i], [load]))
    for piece in pieces:
        for copy in piece[3]:
            copy.start()
    stores = attend(slots_ref, lists_ref, lengths_ref, incoming_ref, blocks, pieces, out_ref, *scratch)
    copy = pltpu.make_async_copy(own_dq_ref, query_grad_ref.at[:, own_cols], own_sems.at[0])
    copy.start()
    for store in stores:
        store.wait()
    copy.wait()


def last_kernel(place_ref, slots_ref, lists_ref, lengths_ref, incoming_ref, *rest):
    late = len(rest) - 8
    message_refs = rest[:late]
    _, dq_ref, out_ref = rest[late : late + 3]
    scratch = rest[late + 3 :]
    parts = lists_ref.shape[0]
    share = message_refs[0].shape[1] // DH
    blocks, pieces = [], []
    for i, message_ref in enumerate(message_refs):
        by = shifts(parts)[parts - 1 - late + i]
        blocks.append(lax.rem(place_ref[0] + parts - by, parts))
        pieces.append((message_ref, message_ref.at[2 * QBLK : 2 * QBLK + 2 * share, 0:DH], dq_ref.at[i], []))
    stores = attend(slots_ref, lists_ref, lengths_ref, incoming_ref, blocks, pieces, out_ref, *scratch)
    for store in stores:
        store.wait()


def place_kernel(place_ref, own_ref, *rest):
    del own_ref
    *piece_refs, out_ref, sems = rest
    parts = len(piece_refs) + 1
    width = out_ref.shape[1] // parts
    copies = []
    for j, piece_ref in enumerate(piece_refs):
        to = lax.rem(place_ref[0] + shifts(parts)[j], parts)
        cols = pl.ds(pl.multiple_of(to * width, width), width)
        copies.append(pltpu.make_async_copy(piece_ref, out_ref.at[:, cols], sems.at[j]))
    for copy in copies:
        copy.start()
    for copy in copies:
        copy.wait()


def sum_kernel(pick_ref, terms_ref, keys_ref, values_ref, total_ref):
    pass_dev, plen, _ = keys_ref.shape
    shards = terms_ref.shape[0]
    blocks = pick_ref.shape[1] // shards
    ways = total_ref.shape[0]
    total_ref[...] = jnp.zeros_like(total_ref)
    for n in range(shards):
        total_ref[n % ways, pick_ref[0, n * blocks]] += terms_ref[slot_of(n)].astype(F32)
    for i in range(pass_dev):
        total = total_ref[0, i + 1]
        for w in range(1, ways):
            total = total + total_ref[w, i + 1]
        keys_ref[i] = total[:plen].astype(BF16)
        values_ref[i] = total[plen:].astype(BF16)


def local(queries, grad_out, attn_out, passage_keys, passage_values, block_lists, passage_lengths):
    shards = lax.axis_size(SHARD_AXES)
    parts = lax.axis_size("tensor")
    my_shard = lax.axis_index(SHARD_AXES)
    place = lax.axis_index("tensor").astype(jnp.int32).reshape(1)
    pass_dev, plen, _ = passage_keys.shape
    rows, columns = queries.shape
    width = columns // parts
    list_len = block_lists.shape[1]
    all_shape = jax.ShapeDtypeStruct((shards, 2 * plen, DH), BF16)

    share = width // DH
    message = jax.ShapeDtypeStruct((2 * QBLK + 2 * share, width), BF16)
    own_shape = jax.ShapeDtypeStruct((2 * share, QBLK), BF16)
    *messages, own_delta = pl.pallas_call(
        prep_kernel,
        out_shape=[message] * (parts - 1) + [own_shape],
        in_specs=[smem(), vmem(), vmem(), vmem()],
        out_specs=[vmem()] * parts,
        scratch_shapes=[pltpu.VMEM((DH, QBLK), F32)],
        compiler_params=params(),
        cost_estimate=pl.CostEstimate(flops=2 * rows * columns, bytes_accessed=10 * rows * columns, transcendentals=0),
        name="prep",
    )(place, queries, grad_out, attn_out)

    def shift(piece, by):
        if by == 0:
            return piece
        return lax.ppermute(piece, "tensor", [(i, (i + by) % parts) for i in range(parts)])

    base = (my_shard * pass_dev).astype(jnp.int32).reshape(1)
    outgoing, pick = pl.pallas_call(
        send_kernel,
        out_shape=[all_shape, jax.ShapeDtypeStruct((1, shards * parts), jnp.int32)],
        in_specs=[smem(), vmem(), vmem(), vmem()],
        out_specs=[vmem(), vmem()],
        compiler_params=params(LARGE_VMEM),
        name="send",
    )(base, block_lists.T, passage_keys, passage_values)
    incoming = exchange(outgoing)
    messages = [shift(piece, by) for piece, by in zip(messages, shifts(parts))]
    own_lists = lax.dynamic_slice_in_dim(block_lists, my_shard * parts, parts, 0)

    own_slots = slot_of(own_lists // pass_dev)
    keys = list_len * plen
    pairs = parts * QBLK * share * keys
    full_shape = jax.ShapeDtypeStruct((rows, columns), BF16)
    piece_shape = (QBLK, width)
    early = parts // 2 - 1
    late = parts - 1 - early

    def scratch(blocks):
        return [
            pltpu.VMEM((blocks, keys, DH), BF16),
            pltpu.VMEM((blocks, keys, DH), BF16),
            pltpu.VMEM((blocks, list_len, 2 * plen, DH), BF16),
            pltpu.VMEM((blocks, keys, DH), F32),
            pltpu.SemaphoreType.DMA((blocks, list_len)),
        ]

    def cost(blocks):
        return pl.CostEstimate(
            flops=10 * pairs * DH * blocks // parts,
            bytes_accessed=8 * rows * width * blocks,
            transcendentals=pairs * blocks // parts,
        )

    query_grad, query_parts, outgoing_grads = pl.pallas_call(
        first_kernel,
        out_shape=[full_shape, jax.ShapeDtypeStruct((early,) + piece_shape, BF16), all_shape],
        in_specs=[smem()] * 4 + [vmem(), hbm(), hbm(), vmem()] + [hbm()] * early,
        out_specs=[hbm(), vmem(), hbm()],
        scratch_shapes=[
            pltpu.VMEM((2 * QBLK, width), BF16),
            pltpu.VMEM((early,) + message.shape, BF16),
            pltpu.VMEM(piece_shape, BF16),
            pltpu.SemaphoreType.DMA((2,)),
            pltpu.SemaphoreType.DMA((early,)),
        ]
        + scratch(early + 1),
        compiler_params=params(),
        cost_estimate=cost(early + 1),
        name="attention_first",
    )(
        place,
        own_slots,
        own_lists,
        passage_lengths,
        incoming,
        in_hbm(queries),
        in_hbm(grad_out),
        own_delta,
        *[in_hbm(piece) for piece in messages[:early]],
    )
    late_parts, outgoing_grads = pl.pallas_call(
        last_kernel,
        out_shape=[jax.ShapeDtypeStruct((late,) + piece_shape, BF16), all_shape],
        in_specs=[smem()] * 4 + [vmem()] * (1 + late) + [hbm()],
        out_specs=[vmem(), hbm()],
        scratch_shapes=scratch(late),
        input_output_aliases={5 + late: 1},
        compiler_params=params(),
        cost_estimate=cost(late),
        name="attention_last",
    )(place, own_slots, own_lists, passage_lengths, incoming, *messages[early:], outgoing_grads)

    returned = exchange(outgoing_grads)
    query_parts = [query_parts[i] for i in range(early)] + [late_parts[i] for i in range(late)]
    query_parts = [shift(piece, parts - by) for piece, by in zip(query_parts, shifts(parts))]
    query_grad = pl.pallas_call(
        place_kernel,
        out_shape=full_shape,
        in_specs=[smem(), hbm()] + [vmem()] * (parts - 1),
        out_specs=hbm(),
        scratch_shapes=[pltpu.SemaphoreType.DMA((parts - 1,))],
        input_output_aliases={1: 0},
        compiler_params=params(),
        cost_estimate=pl.CostEstimate(flops=0, bytes_accessed=4 * rows * columns, transcendentals=0),
        name="place",
    )(place, query_grad, *query_parts)
    grad_shape = jax.ShapeDtypeStruct(passage_keys.shape, BF16)
    key_grad, value_grad = pl.pallas_call(
        sum_kernel,
        out_shape=[grad_shape, grad_shape],
        in_specs=[smem(), vmem()],
        out_specs=[vmem(), vmem()],
        scratch_shapes=[pltpu.VMEM((4, pass_dev + 1, 2 * plen, DH), F32)],
        compiler_params=params(),
        name="sum",
    )(pick, returned)
    return query_grad, key_grad, value_grad


def solution(mesh):
    parts = mesh.shape["tensor"]
    fine = Mesh(mesh.devices.reshape((2,) * len(SHARD_AXES) + (parts,)), SHARD_AXES + ("tensor",))
    tokens = P(SHARD_AXES + ("tensor",), None)
    passages = P(SHARD_AXES, None, "tensor")
    return jax.shard_map(
        local,
        mesh=fine,
        in_specs=(tokens, tokens, tokens, passages, passages, P(), P()),
        out_specs=(tokens, passages, passages),
        check_vma=False,
    )
```

```python
import jax
import jax.numpy as jnp
from jax import lax
from jax.experimental import pallas as pl
from jax.experimental.pallas import tpu as pltpu
from jax.sharding import Mesh
from jax.sharding import PartitionSpec as P

DH = 128
QBLK = 128
BF16 = jnp.bfloat16
F32 = jnp.float32
MASKED = -1e30
LOG2E = 1.4426950408889634
NT = (((1,), (1,)), ((), ()))
TN = (((0,), (0,)), ((), ()))
SMALL_VMEM = 24 * 1024 * 1024
LARGE_VMEM = 60 * 1024 * 1024


SHARD_AXES = ("y2", "y1", "y0", "z2", "z1", "z0", "core")
EXCHANGE_AXES = ("core", "y0", "z0", "y1", "z1", "y2", "z2")


def slot_of(shard):
    bits = len(SHARD_AXES)
    slot = 0
    for i, name in enumerate(EXCHANGE_AXES):
        bit = (shard >> (bits - 1 - SHARD_AXES.index(name))) & 1
        slot = slot | (bit << (bits - 1 - i))
    return slot


def exchange(pieces):
    return lax.all_to_all(pieces, EXCHANGE_AXES, split_axis=0, concat_axis=0, tiled=True)


def shifts(parts):
    far = parts // 2
    return (far,) + tuple(by for by in range(1, parts) if by != far)


def vmem():
    return pl.BlockSpec(memory_space=pltpu.VMEM)


def in_hbm(array):
    return pltpu.with_memory_space_constraint(array, pltpu.HBM)


def hbm():
    return pl.BlockSpec(memory_space=pltpu.HBM)


def smem():
    return pl.BlockSpec(memory_space=pltpu.SMEM)


def params(limit=SMALL_VMEM):
    return pltpu.CompilerParams(vmem_limit_bytes=limit)


def send_kernel(base_ref, lists_ref, keys_ref, values_ref, out_ref, pick_ref):
    pass_dev = keys_ref.shape[0]
    shards = out_ref.shape[0]
    blocks = lists_ref.shape[1] // shards
    here = lists_ref[...] - base_ref[0]
    here = jnp.where((here >= 0) & (here < pass_dev), here + 1, 0)
    here = jnp.sum(here, axis=0, keepdims=True)
    pick = here
    for b in range(1, blocks):
        pick = pick + pltpu.roll(here, here.shape[1] - b, 1)
    pick_ref[...] = pick
    tiles = [jnp.concatenate([keys_ref[i], values_ref[i]], axis=0) for i in range(pass_dev)]
    for n in range(shards):
        k = jnp.broadcast_to(pick[:, n * blocks : n * blocks + 1], tiles[0].shape)
        tile = tiles[0]
        for i in range(1, pass_dev):
            tile = jnp.where(k == i + 1, tiles[i], tile)
        out_ref[slot_of(n)] = tile


def cut_kernel(place_ref, q_ref, g_ref, *message_refs):
    parts = len(message_refs) + 1
    width = q_ref.shape[1] // parts
    for by, message_ref in zip(shifts(parts), message_refs):
        cols = pl.ds(pl.multiple_of(lax.rem(place_ref[0] + by, parts) * width, width), width)
        message_ref[0:QBLK, :] = q_ref[:, cols]
        message_ref[QBLK : 2 * QBLK, :] = g_ref[:, cols]


def delta_kernel(place_ref, g_ref, o_ref, *rest):
    *tile_refs, delta_ref = rest
    parts = len(tile_refs)
    heads = g_ref.shape[1] // DH
    share = heads // parts
    lane = lax.broadcasted_iota(jnp.int32, (QBLK, DH), 1)
    delta = jnp.zeros((QBLK, DH), F32)
    for h in range(heads):
        cols = slice(h * DH, (h + 1) * DH)
        term = jnp.sum(g_ref[:, cols].astype(F32) * o_ref[:, cols].astype(F32), axis=1, keepdims=True)
        delta = jnp.where(lane == h, term, delta)
    delta_ref[...] = delta.T
    for by, tile_ref in zip((0,) + shifts(parts), tile_refs):
        to = lax.rem(place_ref[0] + by, parts)
        rows = delta_ref[pl.ds(pl.multiple_of(to * share, share), share), :]
        high = rows.astype(BF16).astype(F32)
        tile_ref[...] = jnp.concatenate([high, rows - high], axis=0).astype(BF16)


def attend(slots_ref, lists_ref, lengths_ref, incoming_ref, blocks, pieces, out_ref, k_ref, v_ref, terms_ref, bias_ref, sems):
    list_len = lists_ref.shape[1]
    plen = incoming_ref.shape[1] // 2
    share = pieces[0][0].shape[1] // DH
    scale = DH ** (-0.5)
    heads = [slice(h * DH, (h + 1) * DH) for h in range(share)]
    slot_row = lax.broadcasted_iota(jnp.int32, (plen, DH), 0)
    all_slots = []
    for j, block in enumerate(blocks):
        all_slots.append([slots_ref[block, p] for p in range(list_len)])
        for p, slot in enumerate(all_slots[j]):
            rows = slice(p * plen, (p + 1) * plen)
            k_ref[j, rows, :] = incoming_ref[slot, 0:plen, :]
            v_ref[j, rows, :] = incoming_ref[slot, plen : 2 * plen, :]
            bias_ref[j, rows, :] = jnp.where(slot_row < lengths_ref[lists_ref[block, p]], 0.0, MASKED)

    def products(j):
        rows_ref, _, _, loads = pieces[j]
        for copy in loads:
            copy.wait()
        queries = jnp.concatenate([rows_ref[0:QBLK, c] for c in heads], axis=0)
        grads = jnp.concatenate([rows_ref[QBLK : 2 * QBLK, c] for c in heads], axis=0)
        scores = lax.dot_general(k_ref[j], queries, NT, preferred_element_type=F32)
        weight_grads = lax.dot_general(v_ref[j], grads, NT, preferred_element_type=F32)
        return queries, grads, scores, weight_grads

    stores = []
    ahead = products(0)
    for j in range(len(blocks)):
        queries, grads, scores, weight_grads = ahead
        if j + 1 < len(blocks):
            ahead = products(j + 1)
        _, delta_ref, result_ref, _ = pieces[j]
        delta = delta_ref[...].astype(F32)
        delta = delta[:share] + delta[share:]
        delta = jnp.concatenate([delta[h : h + 1] for h in range(share)], axis=1)
        scores = scores * (scale * LOG2E) + jnp.concatenate([bias_ref[j]] * share, axis=1)
        weights = jnp.exp2(scores - jnp.max(scores, axis=0, keepdims=True))
        weights = weights * (1.0 / jnp.sum(weights, axis=0, keepdims=True))
        score_grads = (weights * (weight_grads - delta)).astype(BF16)
        value_term = jnp.dot(weights.astype(BF16), grads, preferred_element_type=F32)
        key_term = jnp.dot(score_grads, queries, preferred_element_type=F32) * scale
        terms_ref[j, :, 0:plen, :] = key_term.astype(BF16).reshape(list_len, plen, DH)
        terms_ref[j, :, plen : 2 * plen, :] = value_term.astype(BF16).reshape(list_len, plen, DH)
        for p, slot in enumerate(all_slots[j]):
            copy = pltpu.make_async_copy(terms_ref.at[j, p], out_ref.at[slot], sems.at[j, p])
            copy.start()
            stores.append(copy)
        query_part = lax.dot_general(k_ref[j], score_grads, TN, preferred_element_type=F32) * scale
        for c in heads:
            result_ref[:, c] = query_part[:, c].T.astype(BF16)
    return stores


def first_kernel(place_ref, slots_ref, lists_ref, lengths_ref, incoming_ref, q_ref, g_ref, own_delta_ref, *rest):
    early = (len(rest) - 12) // 2
    message_refs, delta_refs = rest[:early], rest[early : 2 * early]
    query_grad_ref, dq_ref, out_ref, own_ref, own_dq_ref, own_sems, held_ref, held_sems = rest[2 * early : 2 * early + 8]
    scratch = rest[2 * early + 8 :]
    parts = lists_ref.shape[0]
    width = own_ref.shape[1]
    own_cols = pl.ds(pl.multiple_of(place_ref[0] * width, width), width)
    loads = [
        pltpu.make_async_copy(q_ref.at[:, own_cols], own_ref.at[0:QBLK, :], own_sems.at[0]),
        pltpu.make_async_copy(g_ref.at[:, own_cols], own_ref.at[QBLK : 2 * QBLK, :], own_sems.at[1]),
    ]
    blocks, pieces = [], []
    for i in range(early):
        load = pltpu.make_async_copy(message_refs[i], held_ref.at[i], held_sems.at[i])
        load.start()
        blocks.append(lax.rem(place_ref[0] + parts - shifts(parts)[i], parts))
        pieces.append((held_ref.at[i], delta_refs[i], dq_ref.at[i], [load]))
    for load in loads:
        load.start()
    blocks.append(place_ref[0])
    pieces.append((own_ref, own_delta_ref, own_dq_ref, loads))
    stores = attend(slots_ref, lists_ref, lengths_ref, incoming_ref, blocks, pieces, out_ref, *scratch)
    copy = pltpu.make_async_copy(own_dq_ref, query_grad_ref.at[:, own_cols], own_sems.at[0])
    copy.start()
    for store in stores:
        store.wait()
    copy.wait()


def last_kernel(place_ref, slots_ref, lists_ref, lengths_ref, incoming_ref, *rest):
    late = (len(rest) - 10) // 2
    message_refs, delta_refs = rest[:late], rest[late : 2 * late]
    _, dq_ref, out_ref, held_ref, held_sems = rest[2 * late : 2 * late + 5]
    scratch = rest[2 * late + 5 :]
    parts = lists_ref.shape[0]
    blocks, pieces = [], []
    for i in range(late):
        load = pltpu.make_async_copy(message_refs[i], held_ref.at[i], held_sems.at[i])
        load.start()
        by = shifts(parts)[parts - 1 - late + i]
        blocks.append(lax.rem(place_ref[0] + parts - by, parts))
        pieces.append((held_ref.at[i], delta_refs[i], dq_ref.at[i], [load]))
    stores = attend(slots_ref, lists_ref, lengths_ref, incoming_ref, blocks, pieces, out_ref, *scratch)
    for store in stores:
        store.wait()


def place_kernel(place_ref, own_ref, *rest):
    del own_ref
    *piece_refs, out_ref, sems = rest
    parts = len(piece_refs) + 1
    width = out_ref.shape[1] // parts
    copies = []
    for j, piece_ref in enumerate(piece_refs):
        to = lax.rem(place_ref[0] + shifts(parts)[j], parts)
        cols = pl.ds(pl.multiple_of(to * width, width), width)
        copies.append(pltpu.make_async_copy(piece_ref, out_ref.at[:, cols], sems.at[j]))
    for copy in copies:
        copy.start()
    for copy in copies:
        copy.wait()


def sum_kernel(pick_ref, terms_ref, keys_ref, values_ref, total_ref):
    pass_dev, plen, _ = keys_ref.shape
    shards = terms_ref.shape[0]
    blocks = pick_ref.shape[1] // shards
    ways = total_ref.shape[0]
    total_ref[...] = jnp.zeros_like(total_ref)
    for n in range(shards):
        total_ref[n % ways, pick_ref[0, n * blocks]] += terms_ref[slot_of(n)].astype(F32)
    for i in range(pass_dev):
        total = total_ref[0, i + 1]
        for w in range(1, ways):
            total = total + total_ref[w, i + 1]
        keys_ref[i] = total[:plen].astype(BF16)
        values_ref[i] = total[plen:].astype(BF16)


def local(queries, grad_out, attn_out, passage_keys, passage_values, block_lists, passage_lengths):
    shards = lax.axis_size(SHARD_AXES)
    parts = lax.axis_size("tensor")
    my_shard = lax.axis_index(SHARD_AXES)
    place = lax.axis_index("tensor").astype(jnp.int32).reshape(1)
    pass_dev, plen, _ = passage_keys.shape
    rows, columns = queries.shape
    width = columns // parts
    list_len = block_lists.shape[1]
    all_shape = jax.ShapeDtypeStruct((shards, 2 * plen, DH), BF16)

    share = width // DH
    message = jax.ShapeDtypeStruct((2 * QBLK, width), BF16)
    messages = pl.pallas_call(
        cut_kernel,
        out_shape=[message] * (parts - 1),
        in_specs=[smem(), vmem(), vmem()],
        out_specs=[vmem()] * (parts - 1),
        compiler_params=params(),
        cost_estimate=pl.CostEstimate(flops=0, bytes_accessed=8 * rows * columns, transcendentals=0),
        name="cut",
    )(place, queries, grad_out)
    own_delta, *deltas = pl.pallas_call(
        delta_kernel,
        out_shape=[jax.ShapeDtypeStruct((2 * share, QBLK), BF16)] * parts,
        in_specs=[smem(), vmem(), vmem()],
        out_specs=[vmem()] * parts,
        scratch_shapes=[pltpu.VMEM((DH, QBLK), F32)],
        compiler_params=params(),
        cost_estimate=pl.CostEstimate(flops=2 * rows * columns, bytes_accessed=4 * rows * columns, transcendentals=0),
        name="delta",
    )(place, grad_out, attn_out)

    def shift(piece, by):
        if by == 0:
            return piece
        return lax.ppermute(piece, "tensor", [(i, (i + by) % parts) for i in range(parts)])

    base = (my_shard * pass_dev).astype(jnp.int32).reshape(1)
    outgoing, pick = pl.pallas_call(
        send_kernel,
        out_shape=[all_shape, jax.ShapeDtypeStruct((1, shards * parts), jnp.int32)],
        in_specs=[smem(), vmem(), vmem(), vmem()],
        out_specs=[vmem(), vmem()],
        compiler_params=params(LARGE_VMEM),
        name="send",
    )(base, block_lists.T, passage_keys, passage_values)
    incoming = exchange(outgoing)
    messages = [shift(piece, by) for piece, by in zip(messages, shifts(parts))]
    deltas = [shift(tile, by) for tile, by in zip(deltas, shifts(parts))]
    own_lists = lax.dynamic_slice_in_dim(block_lists, my_shard * parts, parts, 0)

    own_slots = slot_of(own_lists // pass_dev)
    keys = list_len * plen
    pairs = parts * QBLK * share * keys
    full_shape = jax.ShapeDtypeStruct((rows, columns), BF16)
    piece_shape = (QBLK, width)
    early = parts // 2 - 1
    late = parts - 1 - early

    def held(blocks):
        return [pltpu.VMEM((blocks,) + message.shape, BF16), pltpu.SemaphoreType.DMA((blocks,))]

    def scratch(blocks):
        return [
            pltpu.VMEM((blocks, keys, DH), BF16),
            pltpu.VMEM((blocks, keys, DH), BF16),
            pltpu.VMEM((blocks, list_len, 2 * plen, DH), BF16),
            pltpu.VMEM((blocks, keys, DH), F32),
            pltpu.SemaphoreType.DMA((blocks, list_len)),
        ]

    def cost(blocks):
        return pl.CostEstimate(
            flops=10 * pairs * DH * blocks // parts,
            bytes_accessed=8 * rows * width * blocks,
            transcendentals=pairs * blocks // parts,
        )

    query_grad, query_parts, outgoing_grads = pl.pallas_call(
        first_kernel,
        out_shape=[full_shape, jax.ShapeDtypeStruct((early,) + piece_shape, BF16), all_shape],
        in_specs=[smem()] * 4 + [vmem(), hbm(), hbm(), vmem()] + [hbm()] * early + [vmem()] * early,
        out_specs=[hbm(), vmem(), hbm()],
        scratch_shapes=[
            pltpu.VMEM((2 * QBLK, width), BF16),
            pltpu.VMEM(piece_shape, BF16),
            pltpu.SemaphoreType.DMA((2,)),
        ]
        + held(early)
        + scratch(early + 1),
        compiler_params=params(),
        cost_estimate=cost(early + 1),
        name="attention_first",
    )(
        place,
        own_slots,
        own_lists,
        passage_lengths,
        incoming,
        queries,
        grad_out,
        own_delta,
        *messages[:early],
        *deltas[:early],
    )
    late_parts, outgoing_grads = pl.pallas_call(
        last_kernel,
        out_shape=[jax.ShapeDtypeStruct((late,) + piece_shape, BF16), all_shape],
        in_specs=[smem()] * 4 + [vmem()] + [hbm()] * late + [vmem()] * late + [hbm()],
        out_specs=[vmem(), hbm()],
        scratch_shapes=held(late) + scratch(late),
        input_output_aliases={5 + 2 * late: 1},
        compiler_params=params(),
        cost_estimate=cost(late),
        name="attention_last",
    )(place, own_slots, own_lists, passage_lengths, incoming, *messages[early:], *deltas[early:], outgoing_grads)

    returned = exchange(outgoing_grads)
    query_parts = [query_parts[i] for i in range(early)] + [late_parts[i] for i in range(late)]
    query_parts = [shift(piece, parts - by) for piece, by in zip(query_parts, shifts(parts))]
    query_grad = pl.pallas_call(
        place_kernel,
        out_shape=full_shape,
        in_specs=[smem(), hbm()] + [vmem()] * (parts - 1),
        out_specs=hbm(),
        scratch_shapes=[pltpu.SemaphoreType.DMA((parts - 1,))],
        input_output_aliases={1: 0},
        compiler_params=params(),
        cost_estimate=pl.CostEstimate(flops=0, bytes_accessed=4 * rows * columns, transcendentals=0),
        name="place",
    )(place, query_grad, *query_parts)
    grad_shape = jax.ShapeDtypeStruct(passage_keys.shape, BF16)
    key_grad, value_grad = pl.pallas_call(
        sum_kernel,
        out_shape=[grad_shape, grad_shape],
        in_specs=[smem(), vmem()],
        out_specs=[vmem(), vmem()],
        scratch_shapes=[pltpu.VMEM((4, pass_dev + 1, 2 * plen, DH), F32)],
        compiler_params=params(),
        name="sum",
    )(pick, returned)
    return query_grad, key_grad, value_grad


def solution(mesh):
    parts = mesh.shape["tensor"]
    fine = Mesh(mesh.devices.reshape((2,) * len(SHARD_AXES) + (parts,)), SHARD_AXES + ("tensor",))
    tokens = P(SHARD_AXES + ("tensor",), None)
    passages = P(SHARD_AXES, None, "tensor")
    return jax.shard_map(
        local,
        mesh=fine,
        in_specs=(tokens, tokens, tokens, passages, passages, P(), P()),
        out_specs=(tokens, passages, passages),
        check_vma=False,
    )
```

```python
import jax
import jax.numpy as jnp
from jax import lax
from jax.experimental import pallas as pl
from jax.experimental.pallas import tpu as pltpu
from jax.sharding import Mesh
from jax.sharding import PartitionSpec as P

DH = 128
QBLK = 128
BF16 = jnp.bfloat16
F32 = jnp.float32
MASKED = -1e30
LOG2E = 1.4426950408889634
NT = (((1,), (1,)), ((), ()))
TN = (((0,), (0,)), ((), ()))
SMALL_VMEM = 24 * 1024 * 1024
LARGE_VMEM = 60 * 1024 * 1024


SHARD_AXES = ("y2", "y1", "y0", "z2", "z1", "z0", "core")
EXCHANGE_AXES = ("core", "y0", "z0", "y1", "z1", "y2", "z2")


def slot_of(shard):
    bits = len(SHARD_AXES)
    slot = 0
    for i, name in enumerate(EXCHANGE_AXES):
        bit = (shard >> (bits - 1 - SHARD_AXES.index(name))) & 1
        slot = slot | (bit << (bits - 1 - i))
    return slot


def exchange(pieces):
    return lax.all_to_all(pieces, EXCHANGE_AXES, split_axis=0, concat_axis=0, tiled=True)


def shifts(parts):
    far = parts // 2
    return (far,) + tuple(by for by in range(1, parts) if by != far)


def vmem():
    return pl.BlockSpec(memory_space=pltpu.VMEM)


def in_hbm(array):
    return pltpu.with_memory_space_constraint(array, pltpu.HBM)


def hbm():
    return pl.BlockSpec(memory_space=pltpu.HBM)


def smem():
    return pl.BlockSpec(memory_space=pltpu.SMEM)


def params(limit=SMALL_VMEM):
    return pltpu.CompilerParams(vmem_limit_bytes=limit)


def send_kernel(base_ref, lists_ref, keys_ref, values_ref, out_ref, pick_ref):
    pass_dev = keys_ref.shape[0]
    shards = out_ref.shape[0]
    blocks = lists_ref.shape[1] // shards
    here = lists_ref[...] - base_ref[0]
    here = jnp.where((here >= 0) & (here < pass_dev), here + 1, 0)
    here = jnp.sum(here, axis=0, keepdims=True)
    pick = here
    for b in range(1, blocks):
        pick = pick + pltpu.roll(here, here.shape[1] - b, 1)
    pick_ref[...] = pick
    tiles = [jnp.concatenate([keys_ref[i], values_ref[i]], axis=0) for i in range(pass_dev)]
    for n in range(shards):
        k = jnp.broadcast_to(pick[:, n * blocks : n * blocks + 1], tiles[0].shape)
        tile = tiles[0]
        for i in range(1, pass_dev):
            tile = jnp.where(k == i + 1, tiles[i], tile)
        out_ref[slot_of(n)] = tile


def prep_kernel(place_ref, q_ref, g_ref, o_ref, *rest):
    *message_refs, own_ref, delta_ref = rest
    parts = len(message_refs) + 1
    width = q_ref.shape[1] // parts
    share = width // DH
    lane = lax.broadcasted_iota(jnp.int32, (QBLK, DH), 1)
    delta = jnp.zeros((QBLK, DH), F32)
    for h in range(parts * share):
        cols = slice(h * DH, (h + 1) * DH)
        term = jnp.sum(g_ref[:, cols].astype(F32) * o_ref[:, cols].astype(F32), axis=1, keepdims=True)
        delta = jnp.where(lane == h, term, delta)
    delta_ref[...] = delta.T
    for j in range(parts):
        to = lax.rem(place_ref[0] + (0 if j == 0 else shifts(parts)[j - 1]), parts)
        rows = delta_ref[pl.ds(pl.multiple_of(to * share, share), share), :]
        high = rows.astype(BF16).astype(F32)
        rows = jnp.concatenate([high, rows - high], axis=0).astype(BF16)
        if j == 0:
            own_ref[...] = rows
            continue
        message_ref = message_refs[j - 1]
        cols = pl.ds(pl.multiple_of(to * width, width), width)
        message_ref[0:QBLK, :] = q_ref[:, cols]
        message_ref[QBLK : 2 * QBLK, :] = g_ref[:, cols]
        message_ref[2 * QBLK :, :] = jnp.zeros((2 * share, width), BF16)
        message_ref[2 * QBLK :, 0:DH] = rows


def attend(slots_ref, lists_ref, lengths_ref, incoming_ref, blocks, pieces, out_ref, k_ref, v_ref, terms_ref, bias_ref, sems):
    list_len = lists_ref.shape[1]
    plen = incoming_ref.shape[1] // 2
    share = pieces[0][0].shape[1] // DH
    scale = DH ** (-0.5)
    heads = [slice(h * DH, (h + 1) * DH) for h in range(share)]
    slot_row = lax.broadcasted_iota(jnp.int32, (plen, DH), 0)
    all_slots = []
    for j, block in enumerate(blocks):
        all_slots.append([slots_ref[block, p] for p in range(list_len)])
        for p, slot in enumerate(all_slots[j]):
            rows = slice(p * plen, (p + 1) * plen)
            k_ref[j, rows, :] = incoming_ref[slot, 0:plen, :]
            v_ref[j, rows, :] = incoming_ref[slot, plen : 2 * plen, :]
            bias_ref[j, rows, :] = jnp.where(slot_row < lengths_ref[lists_ref[block, p]], 0.0, MASKED)

    def products(j):
        rows_ref, _, _, loads = pieces[j]
        for copy in loads:
            copy.wait()
        queries = jnp.concatenate([rows_ref[0:QBLK, c] for c in heads], axis=0)
        grads = jnp.concatenate([rows_ref[QBLK : 2 * QBLK, c] for c in heads], axis=0)
        scores = lax.dot_general(k_ref[j], queries, NT, preferred_element_type=F32)
        weight_grads = lax.dot_general(v_ref[j], grads, NT, preferred_element_type=F32)
        return queries, grads, scores, weight_grads

    stores = []
    ahead = products(0)
    for j in range(len(blocks)):
        queries, grads, scores, weight_grads = ahead
        if j + 1 < len(blocks):
            ahead = products(j + 1)
        _, delta_ref, result_ref, _ = pieces[j]
        delta = delta_ref[...].astype(F32)
        delta = delta[:share] + delta[share:]
        delta = jnp.concatenate([delta[h : h + 1] for h in range(share)], axis=1)
        scores = scores * (scale * LOG2E) + jnp.concatenate([bias_ref[j]] * share, axis=1)
        weights = jnp.exp2(scores - jnp.max(scores, axis=0, keepdims=True))
        weights = weights * (1.0 / jnp.sum(weights, axis=0, keepdims=True))
        score_grads = (weights * (weight_grads - delta)).astype(BF16)
        value_term = jnp.dot(weights.astype(BF16), grads, preferred_element_type=F32)
        key_term = jnp.dot(score_grads, queries, preferred_element_type=F32) * scale
        terms_ref[j, :, 0:plen, :] = key_term.astype(BF16).reshape(list_len, plen, DH)
        terms_ref[j, :, plen : 2 * plen, :] = value_term.astype(BF16).reshape(list_len, plen, DH)
        for p, slot in enumerate(all_slots[j]):
            copy = pltpu.make_async_copy(terms_ref.at[j, p], out_ref.at[slot], sems.at[j, p])
            copy.start()
            stores.append(copy)
        query_part = lax.dot_general(k_ref[j], score_grads, TN, preferred_element_type=F32) * scale
        for c in heads:
            result_ref[:, c] = query_part[:, c].T.astype(BF16)
    return stores


def first_kernel(place_ref, slots_ref, lists_ref, lengths_ref, incoming_ref, q_ref, g_ref, own_delta_ref, *rest):
    early = len(rest) - 11
    message_refs = rest[:early]
    query_grad_ref, dq_ref, out_ref, own_ref, own_dq_ref, own_sems = rest[early : early + 6]
    scratch = rest[early + 6 :]
    parts = lists_ref.shape[0]
    width = own_ref.shape[1]
    share = width // DH
    own_cols = pl.ds(pl.multiple_of(place_ref[0] * width, width), width)
    loads = [
        pltpu.make_async_copy(q_ref.at[:, own_cols], own_ref.at[0:QBLK, :], own_sems.at[0]),
        pltpu.make_async_copy(g_ref.at[:, own_cols], own_ref.at[QBLK : 2 * QBLK, :], own_sems.at[1]),
    ]
    for load in loads:
        load.start()
    blocks, pieces = [], []
    for i, message_ref in enumerate(message_refs):
        blocks.append(lax.rem(place_ref[0] + parts - shifts(parts)[i], parts))
        pieces.append((message_ref, message_ref.at[2 * QBLK : 2 * QBLK + 2 * share, 0:DH], dq_ref.at[i], []))
    blocks.append(place_ref[0])
    pieces.append((own_ref, own_delta_ref, own_dq_ref, loads))
    stores = attend(slots_ref, lists_ref, lengths_ref, incoming_ref, blocks, pieces, out_ref, *scratch)
    copy = pltpu.make_async_copy(own_dq_ref, query_grad_ref.at[:, own_cols], own_sems.at[0])
    copy.start()
    for store in stores:
        store.wait()
    copy.wait()


def last_kernel(place_ref, slots_ref, lists_ref, lengths_ref, incoming_ref, *rest):
    late = len(rest) - 8
    message_refs = rest[:late]
    _, dq_ref, out_ref = rest[late : late + 3]
    scratch = rest[late + 3 :]
    parts = lists_ref.shape[0]
    share = message_refs[0].shape[1] // DH
    blocks, pieces = [], []
    for i, message_ref in enumerate(message_refs):
        by = shifts(parts)[parts - 1 - late + i]
        blocks.append(lax.rem(place_ref[0] + parts - by, parts))
        pieces.append((message_ref, message_ref.at[2 * QBLK : 2 * QBLK + 2 * share, 0:DH], dq_ref.at[i], []))
    stores = attend(slots_ref, lists_ref, lengths_ref, incoming_ref, blocks, pieces, out_ref, *scratch)
    for store in stores:
        store.wait()


def place_kernel(place_ref, own_ref, *rest):
    del own_ref
    *piece_refs, out_ref, sems = rest
    parts = len(piece_refs) + 1
    width = out_ref.shape[1] // parts
    copies = []
    for j, piece_ref in enumerate(piece_refs):
        to = lax.rem(place_ref[0] + shifts(parts)[j], parts)
        cols = pl.ds(pl.multiple_of(to * width, width), width)
        copies.append(pltpu.make_async_copy(piece_ref, out_ref.at[:, cols], sems.at[j]))
    for copy in copies:
        copy.start()
    for copy in copies:
        copy.wait()


def sum_kernel(pick_ref, terms_ref, keys_ref, values_ref, total_ref):
    pass_dev, plen, _ = keys_ref.shape
    shards = terms_ref.shape[0]
    blocks = pick_ref.shape[1] // shards
    ways = total_ref.shape[0]
    total_ref[...] = jnp.zeros_like(total_ref)
    for n in range(shards):
        total_ref[n % ways, pick_ref[0, n * blocks]] += terms_ref[slot_of(n)].astype(F32)
    for i in range(pass_dev):
        total = total_ref[0, i + 1]
        for w in range(1, ways):
            total = total + total_ref[w, i + 1]
        keys_ref[i] = total[:plen].astype(BF16)
        values_ref[i] = total[plen:].astype(BF16)


def local(queries, grad_out, attn_out, passage_keys, passage_values, block_lists, passage_lengths):
    shards = lax.axis_size(SHARD_AXES)
    parts = lax.axis_size("tensor")
    my_shard = lax.axis_index(SHARD_AXES)
    place = lax.axis_index("tensor").astype(jnp.int32).reshape(1)
    pass_dev, plen, _ = passage_keys.shape
    rows, columns = queries.shape
    width = columns // parts
    list_len = block_lists.shape[1]
    all_shape = jax.ShapeDtypeStruct((shards, 2 * plen, DH), BF16)

    share = width // DH
    message = jax.ShapeDtypeStruct((2 * QBLK + 2 * share, width), BF16)
    own_shape = jax.ShapeDtypeStruct((2 * share, QBLK), BF16)
    *messages, own_delta = pl.pallas_call(
        prep_kernel,
        out_shape=[message] * (parts - 1) + [own_shape],
        in_specs=[smem(), vmem(), vmem(), vmem()],
        out_specs=[vmem()] * parts,
        scratch_shapes=[pltpu.VMEM((DH, QBLK), F32)],
        compiler_params=params(),
        cost_estimate=pl.CostEstimate(flops=2 * rows * columns, bytes_accessed=10 * rows * columns, transcendentals=0),
        name="prep",
    )(place, queries, grad_out, attn_out)

    def shift(piece, by):
        if by == 0:
            return piece
        return lax.ppermute(piece, "tensor", [(i, (i + by) % parts) for i in range(parts)])

    base = (my_shard * pass_dev).astype(jnp.int32).reshape(1)
    outgoing, pick = pl.pallas_call(
        send_kernel,
        out_shape=[all_shape, jax.ShapeDtypeStruct((1, shards * parts), jnp.int32)],
        in_specs=[smem(), vmem(), vmem(), vmem()],
        out_specs=[vmem(), vmem()],
        compiler_params=params(LARGE_VMEM),
        name="send",
    )(base, block_lists.T, passage_keys, passage_values)
    incoming = exchange(outgoing)
    messages = [shift(piece, by) for piece, by in zip(messages, shifts(parts))]
    own_lists = lax.dynamic_slice_in_dim(block_lists, my_shard * parts, parts, 0)

    own_slots = slot_of(own_lists // pass_dev)
    keys = list_len * plen
    pairs = parts * QBLK * share * keys
    full_shape = jax.ShapeDtypeStruct((rows, columns), BF16)
    piece_shape = (QBLK, width)
    early = parts // 2 - 1
    late = parts - 1 - early

    def scratch(blocks):
        return [
            pltpu.VMEM((blocks, keys, DH), BF16),
            pltpu.VMEM((blocks, keys, DH), BF16),
            pltpu.VMEM((blocks, list_len, 2 * plen, DH), BF16),
            pltpu.VMEM((blocks, keys, DH), F32),
            pltpu.SemaphoreType.DMA((blocks, list_len)),
        ]

    def cost(blocks):
        return pl.CostEstimate(
            flops=10 * pairs * DH * blocks // parts,
            bytes_accessed=8 * rows * width * blocks,
            transcendentals=pairs * blocks // parts,
        )

    query_grad, query_parts, outgoing_grads = pl.pallas_call(
        first_kernel,
        out_shape=[full_shape, jax.ShapeDtypeStruct((early,) + piece_shape, BF16), all_shape],
        in_specs=[smem()] * 4 + [vmem(), hbm(), hbm()] + [vmem()] * (1 + early),
        out_specs=[hbm(), vmem(), hbm()],
        scratch_shapes=[
            pltpu.VMEM((2 * QBLK, width), BF16),
            pltpu.VMEM(piece_shape, BF16),
            pltpu.SemaphoreType.DMA((2,)),
        ]
        + scratch(early + 1),
        compiler_params=params(),
        cost_estimate=cost(early + 1),
        name="attention_first",
    )(
        place,
        own_slots,
        own_lists,
        passage_lengths,
        incoming,
        in_hbm(queries),
        in_hbm(grad_out),
        own_delta,
        *messages[:early],
    )
    late_parts, outgoing_grads = pl.pallas_call(
        last_kernel,
        out_shape=[jax.ShapeDtypeStruct((late,) + piece_shape, BF16), all_shape],
        in_specs=[smem()] * 4 + [vmem()] * (1 + late) + [hbm()],
        out_specs=[vmem(), hbm()],
        scratch_shapes=scratch(late),
        input_output_aliases={5 + late: 1},
        compiler_params=params(),
        cost_estimate=cost(late),
        name="attention_last",
    )(place, own_slots, own_lists, passage_lengths, incoming, *messages[early:], outgoing_grads)

    returned = exchange(outgoing_grads)
    query_parts = [query_parts[i] for i in range(early)] + [late_parts[i] for i in range(late)]
    query_parts = [shift(piece, parts - by) for piece, by in zip(query_parts, shifts(parts))]
    query_grad = pl.pallas_call(
        place_kernel,
        out_shape=full_shape,
        in_specs=[smem(), hbm()] + [vmem()] * (parts - 1),
        out_specs=hbm(),
        scratch_shapes=[pltpu.SemaphoreType.DMA((parts - 1,))],
        input_output_aliases={1: 0},
        compiler_params=params(),
        cost_estimate=pl.CostEstimate(flops=0, bytes_accessed=4 * rows * columns, transcendentals=0),
        name="place",
    )(place, query_grad, *query_parts)
    grad_shape = jax.ShapeDtypeStruct(passage_keys.shape, BF16)
    key_grad, value_grad = pl.pallas_call(
        sum_kernel,
        out_shape=[grad_shape, grad_shape],
        in_specs=[smem(), vmem()],
        out_specs=[vmem(), vmem()],
        scratch_shapes=[pltpu.VMEM((4, pass_dev + 1, 2 * plen, DH), F32)],
        compiler_params=params(),
        name="sum",
    )(pick, returned)
    return query_grad, key_grad, value_grad


def solution(mesh):
    parts = mesh.shape["tensor"]
    fine = Mesh(mesh.devices.reshape((2,) * len(SHARD_AXES) + (parts,)), SHARD_AXES + ("tensor",))
    tokens = P(SHARD_AXES + ("tensor",), None)
    passages = P(SHARD_AXES, None, "tensor")
    return jax.shard_map(
        local,
        mesh=fine,
        in_specs=(tokens, tokens, tokens, passages, passages, P(), P()),
        out_specs=(tokens, passages, passages),
        check_vma=False,
    )
```

```python
import jax
import jax.numpy as jnp
from jax import lax
from jax.experimental import pallas as pl
from jax.experimental.pallas import tpu as pltpu
from jax.sharding import Mesh
from jax.sharding import PartitionSpec as P

DH = 128
QBLK = 128
BF16 = jnp.bfloat16
F32 = jnp.float32
MASKED = -1e30
LOG2E = 1.4426950408889634
NT = (((1,), (1,)), ((), ()))
TN = (((0,), (0,)), ((), ()))
SMALL_VMEM = 24 * 1024 * 1024
LARGE_VMEM = 60 * 1024 * 1024


SHARD_AXES = ("y2", "y1", "y0", "z2", "z1", "z0", "core")
EXCHANGE_AXES = ("core", "y0", "z0", "y1", "z1", "y2", "z2")


def slot_of(shard):
    bits = len(SHARD_AXES)
    slot = 0
    for i, name in enumerate(EXCHANGE_AXES):
        bit = (shard >> (bits - 1 - SHARD_AXES.index(name))) & 1
        slot = slot | (bit << (bits - 1 - i))
    return slot


def exchange(pieces):
    return lax.all_to_all(pieces, EXCHANGE_AXES, split_axis=0, concat_axis=0, tiled=True)


def shifts(parts):
    far = parts // 2
    return (far,) + tuple(by for by in range(1, parts) if by != far)


def vmem():
    return pl.BlockSpec(memory_space=pltpu.VMEM)


def in_hbm(array):
    return pltpu.with_memory_space_constraint(array, pltpu.HBM)


def hbm():
    return pl.BlockSpec(memory_space=pltpu.HBM)


def smem():
    return pl.BlockSpec(memory_space=pltpu.SMEM)


def params(limit=SMALL_VMEM):
    return pltpu.CompilerParams(vmem_limit_bytes=limit)


def send_kernel(base_ref, lists_ref, keys_ref, values_ref, out_ref, pick_ref):
    pass_dev = keys_ref.shape[0]
    shards = out_ref.shape[0]
    blocks = lists_ref.shape[1] // shards
    here = lists_ref[...] - base_ref[0]
    here = jnp.where((here >= 0) & (here < pass_dev), here + 1, 0)
    here = jnp.sum(here, axis=0, keepdims=True)
    pick = here
    for b in range(1, blocks):
        pick = pick + pltpu.roll(here, here.shape[1] - b, 1)
    pick_ref[...] = pick
    tiles = [jnp.concatenate([keys_ref[i], values_ref[i]], axis=0) for i in range(pass_dev)]
    for n in range(shards):
        k = jnp.broadcast_to(pick[:, n * blocks : n * blocks + 1], tiles[0].shape)
        tile = tiles[0]
        for i in range(1, pass_dev):
            tile = jnp.where(k == i + 1, tiles[i], tile)
        out_ref[slot_of(n)] = tile


def prep_kernel(place_ref, q_ref, g_ref, o_ref, *rest):
    *message_refs, own_ref, out_ref, delta_ref, sem = rest
    load = pltpu.make_async_copy(o_ref, out_ref, sem)
    load.start()
    parts = len(message_refs) + 1
    width = q_ref.shape[1] // parts
    share = width // DH
    targets = [lax.rem(place_ref[0] + by, parts) for by in (0,) + shifts(parts)]
    for to, message_ref in zip(targets[1:], message_refs):
        cols = pl.ds(pl.multiple_of(to * width, width), width)
        message_ref[0:QBLK, :] = q_ref[:, cols]
        message_ref[QBLK : 2 * QBLK, :] = g_ref[:, cols]
        message_ref[2 * QBLK :, :] = jnp.zeros((2 * share, width), BF16)
    load.wait()
    lane = lax.broadcasted_iota(jnp.int32, (QBLK, DH), 1)
    delta = jnp.zeros((QBLK, DH), F32)
    for h in range(parts * share):
        cols = slice(h * DH, (h + 1) * DH)
        term = jnp.sum(g_ref[:, cols].astype(F32) * out_ref[:, cols].astype(F32), axis=1, keepdims=True)
        delta = jnp.where(lane == h, term, delta)
    delta_ref[...] = delta.T
    for j, to in enumerate(targets):
        rows = delta_ref[pl.ds(pl.multiple_of(to * share, share), share), :]
        high = rows.astype(BF16).astype(F32)
        rows = jnp.concatenate([high, rows - high], axis=0).astype(BF16)
        if j == 0:
            own_ref[...] = rows
        else:
            message_refs[j - 1][2 * QBLK :, 0:DH] = rows


def attend(slots_ref, lists_ref, lengths_ref, incoming_ref, blocks, pieces, out_ref, k_ref, v_ref, terms_ref, bias_ref, sems):
    list_len = lists_ref.shape[1]
    plen = incoming_ref.shape[1] // 2
    share = pieces[0][0].shape[1] // DH
    scale = DH ** (-0.5)
    heads = [slice(h * DH, (h + 1) * DH) for h in range(share)]
    slot_row = lax.broadcasted_iota(jnp.int32, (plen, DH), 0)
    all_slots = []
    for j, block in enumerate(blocks):
        all_slots.append([slots_ref[block, p] for p in range(list_len)])
        for p, slot in enumerate(all_slots[j]):
            rows = slice(p * plen, (p + 1) * plen)
            k_ref[j, rows, :] = incoming_ref[slot, 0:plen, :]
            v_ref[j, rows, :] = incoming_ref[slot, plen : 2 * plen, :]
            bias_ref[j, rows, :] = jnp.where(slot_row < lengths_ref[lists_ref[block, p]], 0.0, MASKED)

    def products(j):
        rows_ref, _, _, loads = pieces[j]
        for copy in loads:
            copy.wait()
        queries = jnp.concatenate([rows_ref[0:QBLK, c] for c in heads], axis=0)
        grads = jnp.concatenate([rows_ref[QBLK : 2 * QBLK, c] for c in heads], axis=0)
        scores = lax.dot_general(k_ref[j], queries, NT, preferred_element_type=F32)
        weight_grads = lax.dot_general(v_ref[j], grads, NT, preferred_element_type=F32)
        return queries, grads, scores, weight_grads

    stores = []
    ahead = products(0)
    for j in range(len(blocks)):
        queries, grads, scores, weight_grads = ahead
        if j + 1 < len(blocks):
            ahead = products(j + 1)
        _, delta_ref, result_ref, _ = pieces[j]
        delta = delta_ref[...].astype(F32)
        delta = delta[:share] + delta[share:]
        delta = jnp.concatenate([delta[h : h + 1] for h in range(share)], axis=1)
        scores = scores * (scale * LOG2E) + jnp.concatenate([bias_ref[j]] * share, axis=1)
        weights = jnp.exp2(scores - jnp.max(scores, axis=0, keepdims=True))
        weights = weights * (1.0 / jnp.sum(weights, axis=0, keepdims=True))
        score_grads = (weights * (weight_grads - delta)).astype(BF16)
        value_term = jnp.dot(weights.astype(BF16), grads, preferred_element_type=F32)
        key_term = jnp.dot(score_grads, queries, preferred_element_type=F32) * scale
        terms_ref[j, :, 0:plen, :] = key_term.astype(BF16).reshape(list_len, plen, DH)
        terms_ref[j, :, plen : 2 * plen, :] = value_term.astype(BF16).reshape(list_len, plen, DH)
        for p, slot in enumerate(all_slots[j]):
            copy = pltpu.make_async_copy(terms_ref.at[j, p], out_ref.at[slot], sems.at[j, p])
            copy.start()
            stores.append(copy)
        query_part = lax.dot_general(k_ref[j], score_grads, TN, preferred_element_type=F32) * scale
        for c in heads:
            result_ref[:, c] = query_part[:, c].T.astype(BF16)
    return stores


def first_kernel(place_ref, slots_ref, lists_ref, lengths_ref, incoming_ref, q_ref, g_ref, own_delta_ref, *rest):
    early = len(rest) - 11
    message_refs = rest[:early]
    query_grad_ref, dq_ref, out_ref, own_ref, own_dq_ref, own_sems = rest[early : early + 6]
    scratch = rest[early + 6 :]
    parts = lists_ref.shape[0]
    width = own_ref.shape[1]
    share = width // DH
    own_cols = pl.ds(pl.multiple_of(place_ref[0] * width, width), width)
    loads = [
        pltpu.make_async_copy(q_ref.at[:, own_cols], own_ref.at[0:QBLK, :], own_sems.at[0]),
        pltpu.make_async_copy(g_ref.at[:, own_cols], own_ref.at[QBLK : 2 * QBLK, :], own_sems.at[1]),
    ]
    for load in loads:
        load.start()
    blocks, pieces = [], []
    for i, message_ref in enumerate(message_refs):
        blocks.append(lax.rem(place_ref[0] + parts - shifts(parts)[i], parts))
        pieces.append((message_ref, message_ref.at[2 * QBLK : 2 * QBLK + 2 * share, 0:DH], dq_ref.at[i], []))
    blocks.append(place_ref[0])
    pieces.append((own_ref, own_delta_ref, own_dq_ref, loads))
    stores = attend(slots_ref, lists_ref, lengths_ref, incoming_ref, blocks, pieces, out_ref, *scratch)
    copy = pltpu.make_async_copy(own_dq_ref, query_grad_ref.at[:, own_cols], own_sems.at[0])
    copy.start()
    for store in stores:
        store.wait()
    copy.wait()


def last_kernel(place_ref, slots_ref, lists_ref, lengths_ref, incoming_ref, *rest):
    late = len(rest) - 8
    message_refs = rest[:late]
    _, dq_ref, out_ref = rest[late : late + 3]
    scratch = rest[late + 3 :]
    parts = lists_ref.shape[0]
    share = message_refs[0].shape[1] // DH
    blocks, pieces = [], []
    for i, message_ref in enumerate(message_refs):
        by = shifts(parts)[parts - 1 - late + i]
        blocks.append(lax.rem(place_ref[0] + parts - by, parts))
        pieces.append((message_ref, message_ref.at[2 * QBLK : 2 * QBLK + 2 * share, 0:DH], dq_ref.at[i], []))
    stores = attend(slots_ref, lists_ref, lengths_ref, incoming_ref, blocks, pieces, out_ref, *scratch)
    for store in stores:
        store.wait()


def place_kernel(place_ref, own_ref, *rest):
    del own_ref
    *piece_refs, out_ref, sems = rest
    parts = len(piece_refs) + 1
    width = out_ref.shape[1] // parts
    copies = []
    for j, piece_ref in enumerate(piece_refs):
        to = lax.rem(place_ref[0] + shifts(parts)[j], parts)
        cols = pl.ds(pl.multiple_of(to * width, width), width)
        copies.append(pltpu.make_async_copy(piece_ref, out_ref.at[:, cols], sems.at[j]))
    for copy in copies:
        copy.start()
    for copy in copies:
        copy.wait()


def sum_kernel(pick_ref, terms_ref, keys_ref, values_ref, total_ref):
    pass_dev, plen, _ = keys_ref.shape
    shards = terms_ref.shape[0]
    blocks = pick_ref.shape[1] // shards
    ways = total_ref.shape[0]
    total_ref[...] = jnp.zeros_like(total_ref)
    for n in range(shards):
        total_ref[n % ways, pick_ref[0, n * blocks]] += terms_ref[slot_of(n)].astype(F32)
    for i in range(pass_dev):
        total = total_ref[0, i + 1]
        for w in range(1, ways):
            total = total + total_ref[w, i + 1]
        keys_ref[i] = total[:plen].astype(BF16)
        values_ref[i] = total[plen:].astype(BF16)


def local(queries, grad_out, attn_out, passage_keys, passage_values, block_lists, passage_lengths):
    shards = lax.axis_size(SHARD_AXES)
    parts = lax.axis_size("tensor")
    my_shard = lax.axis_index(SHARD_AXES)
    place = lax.axis_index("tensor").astype(jnp.int32).reshape(1)
    pass_dev, plen, _ = passage_keys.shape
    rows, columns = queries.shape
    width = columns // parts
    list_len = block_lists.shape[1]
    all_shape = jax.ShapeDtypeStruct((shards, 2 * plen, DH), BF16)

    share = width // DH
    message = jax.ShapeDtypeStruct((2 * QBLK + 2 * share, width), BF16)
    own_shape = jax.ShapeDtypeStruct((2 * share, QBLK), BF16)
    *messages, own_delta = pl.pallas_call(
        prep_kernel,
        out_shape=[message] * (parts - 1) + [own_shape],
        in_specs=[smem(), vmem(), vmem(), hbm()],
        out_specs=[vmem()] * parts,
        scratch_shapes=[pltpu.VMEM((rows, columns), BF16), pltpu.VMEM((DH, QBLK), F32), pltpu.SemaphoreType.DMA],
        compiler_params=params(),
        cost_estimate=pl.CostEstimate(flops=2 * rows * columns, bytes_accessed=10 * rows * columns, transcendentals=0),
        name="prep",
    )(place, queries, grad_out, in_hbm(attn_out))

    def shift(piece, by):
        if by == 0:
            return piece
        return lax.ppermute(piece, "tensor", [(i, (i + by) % parts) for i in range(parts)])

    base = (my_shard * pass_dev).astype(jnp.int32).reshape(1)
    outgoing, pick = pl.pallas_call(
        send_kernel,
        out_shape=[all_shape, jax.ShapeDtypeStruct((1, shards * parts), jnp.int32)],
        in_specs=[smem(), vmem(), vmem(), vmem()],
        out_specs=[vmem(), vmem()],
        compiler_params=params(LARGE_VMEM),
        name="send",
    )(base, block_lists.T, passage_keys, passage_values)
    incoming = exchange(outgoing)
    messages = [shift(piece, by) for piece, by in zip(messages, shifts(parts))]
    own_lists = lax.dynamic_slice_in_dim(block_lists, my_shard * parts, parts, 0)

    own_slots = slot_of(own_lists // pass_dev)
    keys = list_len * plen
    pairs = parts * QBLK * share * keys
    full_shape = jax.ShapeDtypeStruct((rows, columns), BF16)
    piece_shape = (QBLK, width)
    early = parts // 2 - 1
    late = parts - 1 - early

    def scratch(blocks):
        return [
            pltpu.VMEM((blocks, keys, DH), BF16),
            pltpu.VMEM((blocks, keys, DH), BF16),
            pltpu.VMEM((blocks, list_len, 2 * plen, DH), BF16),
            pltpu.VMEM((blocks, keys, DH), F32),
            pltpu.SemaphoreType.DMA((blocks, list_len)),
        ]

    def cost(blocks):
        return pl.CostEstimate(
            flops=10 * pairs * DH * blocks // parts,
            bytes_accessed=8 * rows * width * blocks,
            transcendentals=pairs * blocks // parts,
        )

    query_grad, query_parts, outgoing_grads = pl.pallas_call(
        first_kernel,
        out_shape=[full_shape, jax.ShapeDtypeStruct((early,) + piece_shape, BF16), all_shape],
        in_specs=[smem()] * 4 + [vmem(), hbm(), hbm()] + [vmem()] * (1 + early),
        out_specs=[hbm(), vmem(), hbm()],
        scratch_shapes=[
            pltpu.VMEM((2 * QBLK, width), BF16),
            pltpu.VMEM(piece_shape, BF16),
            pltpu.SemaphoreType.DMA((2,)),
        ]
        + scratch(early + 1),
        compiler_params=params(),
        cost_estimate=cost(early + 1),
        name="attention_first",
    )(
        place,
        own_slots,
        own_lists,
        passage_lengths,
        incoming,
        in_hbm(queries),
        in_hbm(grad_out),
        own_delta,
        *messages[:early],
    )
    late_parts, outgoing_grads = pl.pallas_call(
        last_kernel,
        out_shape=[jax.ShapeDtypeStruct((late,) + piece_shape, BF16), all_shape],
        in_specs=[smem()] * 4 + [vmem()] * (1 + late) + [hbm()],
        out_specs=[vmem(), hbm()],
        scratch_shapes=scratch(late),
        input_output_aliases={5 + late: 1},
        compiler_params=params(),
        cost_estimate=cost(late),
        name="attention_last",
    )(place, own_slots, own_lists, passage_lengths, incoming, *messages[early:], outgoing_grads)

    returned = exchange(outgoing_grads)
    query_parts = [query_parts[i] for i in range(early)] + [late_parts[i] for i in range(late)]
    query_parts = [shift(piece, parts - by) for piece, by in zip(query_parts, shifts(parts))]
    query_grad = pl.pallas_call(
        place_kernel,
        out_shape=full_shape,
        in_specs=[smem(), hbm()] + [vmem()] * (parts - 1),
        out_specs=hbm(),
        scratch_shapes=[pltpu.SemaphoreType.DMA((parts - 1,))],
        input_output_aliases={1: 0},
        compiler_params=params(),
        cost_estimate=pl.CostEstimate(flops=0, bytes_accessed=4 * rows * columns, transcendentals=0),
        name="place",
    )(place, query_grad, *query_parts)
    grad_shape = jax.ShapeDtypeStruct(passage_keys.shape, BF16)
    key_grad, value_grad = pl.pallas_call(
        sum_kernel,
        out_shape=[grad_shape, grad_shape],
        in_specs=[smem(), vmem()],
        out_specs=[vmem(), vmem()],
        scratch_shapes=[pltpu.VMEM((4, pass_dev + 1, 2 * plen, DH), F32)],
        compiler_params=params(),
        name="sum",
    )(pick, returned)
    return query_grad, key_grad, value_grad


def solution(mesh):
    parts = mesh.shape["tensor"]
    fine = Mesh(mesh.devices.reshape((2,) * len(SHARD_AXES) + (parts,)), SHARD_AXES + ("tensor",))
    tokens = P(SHARD_AXES + ("tensor",), None)
    passages = P(SHARD_AXES, None, "tensor")
    return jax.shard_map(
        local,
        mesh=fine,
        in_specs=(tokens, tokens, tokens, passages, passages, P(), P()),
        out_specs=(tokens, passages, passages),
        check_vma=False,
    )
```
